32 devices in a mesh: fsdp: 4 (over y, x), seq: 8 (over z, core).
Axes of the slice: x: 2, y: 2, z: 4, core: 2. Of those that a mesh axis runs over, the one named last changes fastest.
Arguments:
- tokens: bfloat16 [2, 4, 1024, 2048], P(None, 'fsdp', 'seq'), may hold values from -6 to 6
- cotangent: bfloat16 [2, 4, 1024, 2048], P(None, 'fsdp', 'seq'), may hold values from -6 to 6
- piece_starts: int32 [2, 4, 2], P(None, 'fsdp'), may hold values from 0 to 768, as said below
- attn_blocks: float32 [1024, 12, 1024], P(('fsdp', 'seq'))
- ffn_blocks: float32 [1024, 48, 1024], P(('fsdp', 'seq'))
- gains: float32 [2, 2048], P(None, ('fsdp', 'seq')), may hold values from 0.5 to 1.5
- left_stats: float32 [64, 1024, 1024], P(('fsdp', 'seq'))
- right_stats: float32 [64, 1024, 1024], P(('fsdp', 'seq'))
- left_root: float32 [64, 1024, 1024], P(('fsdp', 'seq'))
- right_root: float32 [64, 1024, 1024], P(('fsdp', 'seq'))
- owner_slot: int32 [60], replicated, may hold values from 0 to 63, as said below
Outputs:
- block_out: bfloat16 [2, 4, 1024, 2048], P(None, 'fsdp', 'seq')
- input_grad: bfloat16 [2, 4, 1024, 2048], P(None, 'fsdp', 'seq')
- attn_grad: float32 [1024, 12, 1024], P(('fsdp', 'seq'))
- ffn_grad: float32 [1024, 48, 1024], P(('fsdp', 'seq'))
- gain_grad: float32 [2, 2048], P(None, ('fsdp', 'seq'))
- new_attn: float32 [1024, 12, 1024], P(('fsdp', 'seq'))
- new_ffn: float32 [1024, 48, 1024], P(('fsdp', 'seq'))
- new_gains: float32 [2, 2048], P(None, ('fsdp', 'seq'))
- new_left: float32 [64, 1024, 1024], P(('fsdp', 'seq'))
- new_right: float32 [64, 1024, 1024], P(('fsdp', 'seq'))
The draws below stay inside these ranges and needn't reach their ends.
Inputs may be any that keep to these rules, and one draw needn't show every extreme that they name: `piece_starts`: in each sequence the 2 pieces of 256 positions start in rising order, do not intersect and lie inside the sequence. `owner_slot`: all entries differ; slot s lies on device s // 2 of fsdp+seq, as its index 2 s + k.
All inputs are finite; a program needn't handle non-finite values.
Results may differ from the reference program's by a relative error of at most 0.018.
The reference program's roundings to bfloat16 on the way count: a program that leaves them out, or rounds other values in their place, can miss the bound.
Values may be sent and summed in bfloat16 or wider, within the bound.
A program may use at most 896 MiB of HBM per device.

```python
import math
import jax
import jax.numpy as jnp
from jax import lax

D = 2048
QUERY_HEADS = 16
KEY_VALUE_HEADS = 8
HEAD_SIZE = 128
FF = 8192
PRECOND_ORDER = 1024
MICRO = 2
PIECE = 256
PICS = 2
SEQUENCE_LENGTH = 1024
SEQS = 4
TOKENS = 8192
ATT_BLK = 12
FFN_BLK = 48
NBLK = 60
SLOTS_ALL = 64


def kind_table(pairs):
    return jnp.concatenate([jnp.full((block_count,), block_value, jnp.float32) for block_count, block_value in pairs])


def attention_reach():
    length = 1.0 * SEQUENCE_LENGTH
    ratio = max(length / 55.0, 1.0)
    return max(1.0, length / (55.0 * (1.0 + math.log(ratio))))


def block_kinds():
    model_blocks = D // PRECOND_ORDER
    head_blocks = QUERY_HEADS * HEAD_SIZE // PRECOND_ORDER
    query_group_blocks = KEY_VALUE_HEADS * HEAD_SIZE // PRECOND_ORDER
    feed_blocks = FF // PRECOND_ORDER
    reach = attention_reach()
    output_spread = 0.5 * (reach / (QUERY_HEADS * HEAD_SIZE)) ** 0.5
    spreads = kind_table([(model_blocks * head_blocks, 1.2 * D ** (-0.5)), (model_blocks * query_group_blocks, 1.67 * D ** (-0.5)), (model_blocks * query_group_blocks, D ** (-0.5)), (head_blocks * model_blocks, output_spread), (2 * model_blocks * feed_blocks, D ** (-0.5)), (feed_blocks * model_blocks, 2.0 * FF ** (-0.5))])
    squares = kind_table([(model_blocks * head_blocks, 0.9), (model_blocks * query_group_blocks, 0.9), (model_blocks * query_group_blocks, 0.7), (head_blocks * model_blocks, min(1.5, 2.7 / reach)), (model_blocks * feed_blocks, 0.3), (model_blocks * feed_blocks, 0.35), (feed_blocks * model_blocks, 0.35)])
    return (spreads, squares)


def assignment(key):
    key = jax.random.fold_in(key, 101)
    first_key, second_key = jax.random.split(key)
    middle = jax.random.permutation(first_key, SLOTS_ALL - 2)[:NBLK - 2] + 1
    listed = jnp.concatenate([jnp.array([0, SLOTS_ALL - 1], jnp.int32), middle.astype(jnp.int32)])
    return listed[jax.random.permutation(second_key, NBLK)]


def slot_kinds(key):
    owners = assignment(key)
    spreads, squares = block_kinds()
    slot_match = owners[None, :] == jnp.arange(SLOTS_ALL).astype(jnp.int32)[:, None]
    filled = jnp.any(slot_match, axis=1)
    slot_spread = jnp.where(filled, jnp.sum(jnp.where(slot_match, spreads[None, :], 0.0), axis=1), D ** (-0.5))
    slot_square = jnp.where(filled, jnp.sum(jnp.where(slot_match, squares[None, :], 0.0), axis=1), 0.5)
    return (slot_spread, slot_square)


def diagonal_of(entries):
    return jnp.eye(PRECOND_ORDER, dtype=jnp.float32)[None] * entries[:, None, :]


def root_matrix(level, noise, slot_spread, slot_square):
    size_slot = (slot_square * TOKENS) ** (-0.25) * jnp.sqrt(slot_spread)
    mixing = (noise + jnp.transpose(noise, (0, 2, 1))) * (0.25 / (2.0 * PRECOND_ORDER) ** 0.5)
    return (mixing + diagonal_of(0.7 * jnp.exp2(level))) * size_slot[:, None, None]


def draw_owner_slot(key, part):
    return assignment(key)


def draw_piece_starts(key, part):
    key = jax.random.fold_in(key, 7)
    first_key, second_key = jax.random.split(key)
    spare = SEQUENCE_LENGTH - PICS * PIECE
    offsets = jnp.sort(jax.random.randint(first_key, (MICRO * SEQS, PICS), 0, spare + 1), axis=-1)
    chosen = jax.random.randint(second_key, (), 0, MICRO * SEQS)
    row_ids = jnp.arange(MICRO * SEQS)
    offsets = offsets.at[:, 0].set(jnp.where(row_ids == chosen, 0, offsets[:, 0]))
    offsets = offsets.at[:, -1].set(jnp.where(row_ids == chosen, spare, offsets[:, -1]))
    starts = offsets + jnp.arange(PICS)[None, :] * PIECE
    return starts.reshape(MICRO, SEQS, PICS).astype(jnp.int32)


def draw_attn_blocks(key, part):
    key = jax.random.fold_in(key, 5)
    spreads, squares = block_kinds()
    noise = jax.random.normal(key, (PRECOND_ORDER, ATT_BLK, PRECOND_ORDER))
    return noise * spreads[None, :ATT_BLK, None]


def draw_ffn_blocks(key, part):
    key = jax.random.fold_in(key, 6)
    spreads, squares = block_kinds()
    noise = jax.random.normal(key, (PRECOND_ORDER, FFN_BLK, PRECOND_ORDER))
    return noise * spreads[None, ATT_BLK:, None]


def draw_left_stats(key, part):
    slot_spread, slot_square = slot_kinds(key)
    key = jax.random.fold_in(key, 2)
    level = jax.random.uniform(key, (SLOTS_ALL, PRECOND_ORDER))
    factor = jnp.exp2(2.0 * level)
    return diagonal_of(factor * slot_square[:, None])


def draw_right_stats(key, part):
    slot_spread, slot_square = slot_kinds(key)
    key = jax.random.fold_in(key, 3)
    level = jax.random.uniform(key, (SLOTS_ALL, PRECOND_ORDER))
    factor = jnp.exp2(2.0 * level)
    return diagonal_of(factor * slot_square[:, None])


def draw_left_root(key, part):
    slot_spread, slot_square = slot_kinds(key)
    key = jax.random.fold_in(key, 4)
    first_key, second_key = jax.random.split(key)
    level = jax.random.uniform(first_key, (SLOTS_ALL, PRECOND_ORDER))
    noise = jax.random.normal(second_key, (SLOTS_ALL, PRECOND_ORDER, PRECOND_ORDER))
    return root_matrix(level, noise, slot_spread, slot_square)


def draw_right_root(key, part):
    slot_spread, slot_square = slot_kinds(key)
    key = jax.random.fold_in(key, 8)
    first_key, second_key = jax.random.split(key)
    level = jax.random.uniform(first_key, (SLOTS_ALL, PRECOND_ORDER))
    noise = jax.random.normal(second_key, (SLOTS_ALL, PRECOND_ORDER, PRECOND_ORDER))
    return root_matrix(level, noise, slot_spread, slot_square)


def steps_of(rng, extent, cuts, smallest, top_value):
    def one(dim, blocks):
        heights = jax.random.uniform(jax.random.fold_in(jax.random.fold_in(rng, 6), dim), (blocks,), jnp.float32, smallest / len(cuts), top_value / len(cuts))
        return jnp.repeat(jnp.exp(heights), extent[dim] // blocks).reshape((-1,) + (1,) * (len(extent) - dim - 1))

    loudness = one(*cuts[0])
    for cut in cuts[1:]:
        loudness = loudness * one(*cut)
    return loudness


def centred(own_key, shape, scale, limit, cuts=(), kind=jnp.bfloat16):
    drawn = jax.random.normal(own_key, shape, jnp.float32) * scale
    if len(cuts) > 0:
        drawn = steps_of(own_key, shape, cuts, -0.22, 0.18) * drawn
    return jnp.clip(drawn, min=-limit, max=limit).astype(kind)


def setup_inputs(seed: int = 0) -> dict:
    key_list = jax.random.split(jax.random.key(seed), 12)
    return {
        "tokens": centred(key_list[0], (MICRO, SEQS, SEQUENCE_LENGTH, D), 1.0, 6.0, ((1, 4), (2, 8))),
        "cotangent": centred(key_list[1], (MICRO, SEQS, SEQUENCE_LENGTH, D), 1.0, 6.0, ((1, 4), (2, 8))),
        "piece_starts": draw_piece_starts(jax.random.fold_in(key_list[11], 71), 0),
        "attn_blocks": draw_attn_blocks(jax.random.fold_in(key_list[11], 71), 0),
        "ffn_blocks": draw_ffn_blocks(jax.random.fold_in(key_list[11], 71), 0),
        "gains": jnp.clip(1.0 + 0.1 * jax.random.normal(key_list[5], (2, D), jnp.float32), 0.5, 1.5),
        "left_stats": draw_left_stats(jax.random.fold_in(key_list[11], 71), 0),
        "right_stats": draw_right_stats(jax.random.fold_in(key_list[11], 71), 0),
        "left_root": draw_left_root(jax.random.fold_in(key_list[11], 71), 0),
        "right_root": draw_right_root(jax.random.fold_in(key_list[11], 71), 0),
        "owner_slot": draw_owner_slot(jax.random.fold_in(key_list[11], 71), 0),
    }


EPSILON = 1e-06
ROTARY_BASE = 1000000.0
STAT_DECAY = 0.5
STEP_RATE = 1.0
GAIN_RATE = 0.001
EXACT_PRECISION = lax.Precision.HIGHEST

@jax.custom_vjp
def low(v):
    return lax.optimization_barrier(v.astype(jnp.bfloat16)).astype(jnp.float32)

@jax.custom_vjp
def low_back(v):
    return v

def low_keep(v):
    return (low(v), None)

def low_pass(kept, grad):
    return (grad,)

def back_keep(v):
    return (v, None)

def back_low(kept, grad):
    return (low(grad),)
low.defvjp(low_keep, low_pass)
low_back.defvjp(back_keep, back_low)

def assemble(blocks, offset, row_blocks, col_blocks):
    part = blocks[:, offset:offset + row_blocks * col_blocks, :].reshape(PRECOND_ORDER, row_blocks, col_blocks, PRECOND_ORDER)
    return jnp.transpose(part, (1, 0, 2, 3)).reshape(row_blocks * PRECOND_ORDER, col_blocks * PRECOND_ORDER)

def matrices_of(attn_low, ffn_low):
    model_blocks = D // PRECOND_ORDER
    head_blocks = QUERY_HEADS * HEAD_SIZE // PRECOND_ORDER
    query_group_blocks = KEY_VALUE_HEADS * HEAD_SIZE // PRECOND_ORDER
    feed_blocks = FF // PRECOND_ORDER
    return (assemble(attn_low, 0, model_blocks, head_blocks), assemble(attn_low, model_blocks * head_blocks, model_blocks, query_group_blocks), assemble(attn_low, model_blocks * (head_blocks + query_group_blocks), model_blocks, query_group_blocks), assemble(attn_low, model_blocks * (head_blocks + 2 * query_group_blocks), head_blocks, model_blocks), assemble(ffn_low, 0, model_blocks, feed_blocks), assemble(ffn_low, model_blocks * feed_blocks, model_blocks, feed_blocks), assemble(ffn_low, 2 * model_blocks * feed_blocks, feed_blocks, model_blocks))

def rotary_embedding(value_matrix, token_positions):
    half_dim = HEAD_SIZE // 2
    frequency = jnp.power(ROTARY_BASE, -(jnp.arange(half_dim).astype(jnp.float32) * (2.0 / HEAD_SIZE)))
    angles = token_positions.astype(jnp.float32)[:, None] * frequency[None, :]
    cosine_values = jnp.cos(angles)[:, None, :]
    sine_values = jnp.sin(angles)[:, None, :]
    first_half = value_matrix[..., :half_dim]
    second = value_matrix[..., half_dim:]
    return jnp.concatenate([first_half * cosine_values - second * sine_values, second * cosine_values + first_half * sine_values], axis=-1)

def allowed_pairs(starts, query_pos, key_pos):
    ending = starts + PIECE
    query_in = (query_pos[:, None] >= starts[None, :]) & (query_pos[:, None] < ending[None, :])
    key_in = (key_pos[:, None] >= starts[None, :]) & (key_pos[:, None] < ending[None, :])
    shared = jnp.dot(query_in.astype(jnp.float32), key_in.astype(jnp.float32).T) > 0.5
    return (key_pos[None, :] <= query_pos[:, None]) | shared

def one_sequence(tokens_row, starts, weights, gain_pair):
    query_w, key_w, value_weight, out_w, gate_w, up_w, down_w = weights
    token_positions = jnp.arange(SEQUENCE_LENGTH).astype(jnp.int32)
    score_scale = HEAD_SIZE ** (-0.5)
    queries_per_group = QUERY_HEADS // KEY_VALUE_HEADS
    inv_one = lax.rsqrt(lax.optimization_barrier(jnp.mean(tokens_row * tokens_row, axis=-1, keepdims=True)) + EPSILON)
    normalized_input = low(tokens_row * inv_one * gain_pair[0])
    query_matrix = low_back(jnp.dot(normalized_input, query_w, precision=EXACT_PRECISION))
    key_lines = low_back(jnp.dot(normalized_input, key_w, precision=EXACT_PRECISION))
    value_matrix = low(low_back(jnp.dot(normalized_input, value_weight, precision=EXACT_PRECISION))).reshape(SEQUENCE_LENGTH, KEY_VALUE_HEADS, HEAD_SIZE)
    query_matrix = low(rotary_embedding(query_matrix.reshape(SEQUENCE_LENGTH, QUERY_HEADS, HEAD_SIZE), token_positions)).reshape(SEQUENCE_LENGTH, KEY_VALUE_HEADS, queries_per_group, HEAD_SIZE)
    key_lines = low(rotary_embedding(key_lines.reshape(SEQUENCE_LENGTH, KEY_VALUE_HEADS, HEAD_SIZE), token_positions))
    query_block = min(512, SEQUENCE_LENGTH)

    def attend(number):
        first_row = number * query_block
        block_queries = lax.dynamic_slice_in_dim(query_matrix, first_row, query_block, 0)
        block_pos = first_row + jnp.arange(query_block).astype(jnp.int32)
        allowed = allowed_pairs(starts, block_pos, token_positions)
        scores = low_back(jnp.einsum('qhgd,khd->hgqk', block_queries, key_lines, precision=EXACT_PRECISION) * score_scale)
        scores = jnp.where(allowed[None, None], scores, -1e+30)
        top_score = lax.optimization_barrier(jnp.max(scores, axis=-1, keepdims=True))
        exponent = jnp.exp(scores - top_score)
        chances = low(exponent / lax.optimization_barrier(jnp.sum(exponent, axis=-1, keepdims=True)))
        return jnp.einsum('hgqk,khd->qhgd', chances, value_matrix, precision=EXACT_PRECISION)
    mixed_heads = lax.map(jax.checkpoint(attend), jnp.arange(SEQUENCE_LENGTH // query_block).astype(jnp.int32))
    mixed_heads = low(low_back(mixed_heads.reshape(SEQUENCE_LENGTH, QUERY_HEADS * HEAD_SIZE)))
    hidden_one = tokens_row + low_back(jnp.dot(mixed_heads, out_w, precision=EXACT_PRECISION))
    inv_two = lax.rsqrt(lax.optimization_barrier(jnp.mean(hidden_one * hidden_one, axis=-1, keepdims=True)) + EPSILON)
    normed_two = low(hidden_one * inv_two * gain_pair[1])
    gate_act = low_back(jnp.dot(normed_two, gate_w, precision=EXACT_PRECISION))
    upward = low_back(jnp.dot(normed_two, up_w, precision=EXACT_PRECISION))
    inner_act = low(gate_act * jax.nn.sigmoid(gate_act) * upward)
    return hidden_one + jnp.dot(inner_act, down_w, precision=EXACT_PRECISION)

def forward_all(tokens_f, attn_blocks, ffn_blocks, gains, piece_starts):
    weights = matrices_of(low(attn_blocks), low(ffn_blocks))
    gain_low = low(gains)
    flat_tokens = tokens_f.reshape(MICRO * SEQS, SEQUENCE_LENGTH, D)
    flat_starts = piece_starts.reshape(MICRO * SEQS, PICS)
    checked = jax.checkpoint(one_sequence)

    def sequence_step(entry):
        return checked(entry[0], entry[1], weights, gain_low)
    return lax.map(sequence_step, (flat_tokens, flat_starts)).reshape(MICRO, SEQS, SEQUENCE_LENGTH, D)

def reference(tokens, cotangent, piece_starts, attn_blocks, ffn_blocks, gains, left_stats, right_stats, left_root, right_root, owner_slot):

    def forward_only(tokens_f, attn_f, ffn_f, gains_f):
        return forward_all(tokens_f, attn_f, ffn_f, gains_f, piece_starts)
    block_out, pullback = jax.vjp(forward_only, tokens.astype(jnp.float32), attn_blocks, ffn_blocks, gains)
    input_grad, attn_grad, ffn_grad, gain_grad = pullback(cotangent.astype(jnp.float32))
    grads_all = jnp.concatenate([attn_grad, ffn_grad], axis=1)
    masters = jnp.concatenate([attn_blocks, ffn_blocks], axis=1)
    by_block = jnp.transpose(grads_all, (1, 0, 2))
    slot_ids = jnp.arange(SLOTS_ALL).astype(jnp.int32)
    slot_match = owner_slot[None, :] == slot_ids[:, None]
    filled = jnp.any(slot_match, axis=1)
    slot_block = lax.optimization_barrier(jnp.sum(jnp.where(slot_match, jnp.arange(NBLK).astype(jnp.int32)[None, :], 0), axis=1))
    held_grad = jnp.where(filled[:, None, None], by_block[slot_block], 0.0)
    normalizer = 1.0 * TOKENS * PRECOND_ORDER
    gram_left = jnp.einsum('sij,skj->sik', held_grad, held_grad, precision=EXACT_PRECISION) / normalizer
    gram_right = jnp.einsum('sji,sjk->sik', held_grad, held_grad, precision=EXACT_PRECISION) / normalizer
    new_left = jnp.where(filled[:, None, None], STAT_DECAY * left_stats + (1.0 - STAT_DECAY) * gram_left, left_stats)
    new_right = jnp.where(filled[:, None, None], STAT_DECAY * right_stats + (1.0 - STAT_DECAY) * gram_right, right_stats)
    left_part = jnp.einsum('sij,sjk->sik', left_root, held_grad, precision=EXACT_PRECISION)
    precond = jnp.einsum('sij,sjk->sik', left_part, right_root, precision=EXACT_PRECISION)
    update = jnp.transpose(precond[owner_slot], (1, 0, 2))
    new_master = masters - STEP_RATE * update
    new_gains = gains - GAIN_RATE * gain_grad
    return (block_out.astype(jnp.bfloat16), input_grad.astype(jnp.bfloat16), attn_grad, ffn_grad, gain_grad, new_master[:, :ATT_BLK], new_master[:, ATT_BLK:], new_gains, new_left, new_right)
```

```python
import functools

import jax
import jax.numpy as jnp
from jax import lax
from jax.experimental import pallas as pl
from jax.experimental.pallas import tpu as pltpu
from jax.sharding import PartitionSpec as P

D = 2048
QUERY_HEADS = 16
KEY_VALUE_HEADS = 8
HEAD_SIZE = 128
FF = 8192
PRECOND_ORDER = 1024
MICRO = 2
PIECE = 256

EPSILON = 1e-06
ROTARY_BASE = 1000000.0
STAT_DECAY = 0.5
STEP_RATE = 1.0
GAIN_RATE = 0.001

F32 = jnp.float32
BF16 = jnp.bfloat16
BOTH = ("fsdp", "seq")
SCALE = HEAD_SIZE ** (-0.5)
QUERY_ROWS = 256
D_BLK = D // PRECOND_ORDER
FF_BLK = FF // PRECOND_ORDER
VMEM_LIMIT = 56 * 1024 * 1024


def dot(a, b, contract):
    return lax.dot_general(a, b, (contract, ((), ())), preferred_element_type=F32)


def nn(a, b):
    return dot(a, b, ((1,), (0,)))


def nt(a, b):
    return dot(a, b, ((1,), (1,)))


def tn(a, b):
    return dot(a, b, ((0,), (0,)))


def swap_seq(array, axis):
    return lax.all_to_all(array, "seq", split_axis=axis, concat_axis=axis, tiled=True)


def column_parts(shard, parts):
    rows = shard.shape[0]
    columns = shard.shape[1] // D_BLK * PRECOND_ORDER // parts
    return shard.reshape(rows, D_BLK, parts, columns).transpose(2, 1, 0, 3)


def gather_columns(parts):
    swapped = swap_seq(parts, 0)
    whole = lax.all_gather(swapped, "fsdp", axis=0, tiled=False)
    return whole.transpose(2, 0, 1, 3, 4).reshape(D, parts.shape[-1])


def scatter_columns(term, rows):
    seq, fsdp = lax.axis_size("seq"), lax.axis_size("fsdp")
    shaped = term.astype(BF16).reshape(D_BLK, fsdp, seq, rows, term.shape[1]).transpose(1, 0, 2, 3, 4)
    summed = lax.psum_scatter(shaped, "fsdp", scatter_dimension=0, tiled=False)
    return swap_seq(summed, 1)


def gather_rows(shard):
    seq, fsdp = lax.axis_size("seq"), lax.axis_size("fsdp")
    rows, groups = shard.shape[:2]
    by_group = shard.reshape(rows, groups, D).transpose(1, 0, 2)
    if groups == seq:
        swapped = swap_seq(by_group, 0)
        whole = lax.all_gather(swapped, "fsdp", axis=0, tiled=False)
        return whole.reshape(PRECOND_ORDER, D)
    whole = lax.all_gather(by_group, "fsdp", axis=1, tiled=False)
    pieces = whole.reshape(seq, groups * fsdp // seq, rows, D)
    swapped = swap_seq(pieces, 0)
    return swapped.transpose(1, 0, 2, 3).reshape(groups * PRECOND_ORDER // seq, D)


def scatter_rows(term, rows):
    seq, fsdp = lax.axis_size("seq"), lax.axis_size("fsdp")
    groups = term.shape[0] * seq // PRECOND_ORDER
    term = term.astype(BF16)
    if groups == seq:
        summed = lax.psum_scatter(
            term.reshape(fsdp, seq, rows, D), "fsdp", scatter_dimension=0, tiled=False
        )
        return swap_seq(summed, 0)
    pieces = term.reshape(groups * fsdp // seq, seq, rows, D).transpose(1, 0, 2, 3)
    swapped = swap_seq(pieces, 0).reshape(groups, fsdp, rows, D).transpose(1, 0, 2, 3)
    return lax.psum_scatter(swapped, "fsdp", scatter_dimension=0, tiled=False)


def turn(value, cosine, sine, sign):
    return value * cosine + sign * (pltpu.roll(value, HEAD_SIZE // 2, 1) * sine)


def piece_index(starts_ref, micro, position, outside):
    index = jnp.full(position.shape, outside, jnp.int32)
    for piece in range(starts_ref.shape[1]):
        start = starts_ref[micro, piece]
        index = jnp.where((position >= start) & (position < start + PIECE), piece, index)
    return index


def softmax_rows(queries, keys, starts_ref, micro, first):
    rows, length = queries.shape[0], keys.shape[0]
    query_pos = first + lax.broadcasted_iota(jnp.int32, (rows, 1), 0)
    key_pos = lax.broadcasted_iota(jnp.int32, (1, length), 1)
    same = piece_index(starts_ref, micro, query_pos, -1) == piece_index(
        starts_ref, micro, key_pos, -2
    )
    scores = jnp.where((key_pos <= query_pos) | same, nt(queries, keys) * SCALE, -1e30)
    exponent = jnp.exp(scores - jnp.max(scores, axis=1, keepdims=True))
    return exponent / jnp.sum(exponent, axis=1, keepdims=True)


def query_blocks(length):
    rows = min(QUERY_ROWS, length)
    for first in range(0, length, rows):
        yield first, rows, min(length, first + rows + PIECE)


def attend_kernel(heads, starts_ref, qkv_ref, cosine_ref, sine_ref, kept_ref, mixed_ref, k_ref, v_ref):
    micro = pl.program_id(0)
    parts, _, rows, _ = qkv_ref.shape
    length = parts * rows
    cosine, sine = cosine_ref[...], sine_ref[...]

    def columns(head):
        return pl.ds(head * HEAD_SIZE, HEAD_SIZE)

    def turned(head):
        value = qkv_ref[:, 0, :, columns(head)].reshape(length, HEAD_SIZE)
        return turn(value, cosine, sine, 1.0).astype(BF16)

    def keep(head, value):
        kept_ref[:, 0, :, columns(head)] = value.reshape(parts, rows, HEAD_SIZE)

    k_ref[...] = turned(heads)
    v_ref[...] = qkv_ref[:, 0, :, columns(heads + 1)].reshape(length, HEAD_SIZE).astype(BF16)
    keep(heads, k_ref[...])
    keep(heads + 1, v_ref[...])
    for head in range(heads):
        queries = turned(head)
        keep(head, queries)
        for first, count, seen in query_blocks(length):
            chances = softmax_rows(
                queries[first : first + count], k_ref[:seen], starts_ref, micro, first
            )
            mixed = nn(chances.astype(BF16), v_ref[:seen]).astype(BF16)
            mixed_ref[first // rows : (first + count) // rows, 0, :, columns(head)] = mixed.reshape(
                count // rows, rows, HEAD_SIZE
            )


def attend_back_kernel(
    heads, starts_ref, kept_ref, grad_ref, cosine_ref, sine_ref, q_out, kv_out, k_acc, v_acc
):
    micro = pl.program_id(0)
    parts, _, rows, _ = kept_ref.shape
    length = parts * rows

    def columns(head):
        return pl.ds(head * HEAD_SIZE, HEAD_SIZE)

    keys = kept_ref[:, 0, :, columns(heads)].reshape(length, HEAD_SIZE)
    values = kept_ref[:, 0, :, columns(heads + 1)].reshape(length, HEAD_SIZE)
    k_acc[...] = jnp.zeros_like(k_acc)
    v_acc[...] = jnp.zeros_like(v_acc)
    for head in range(heads):
        for first, count, seen in query_blocks(length):
            span = slice(first // rows, (first + count) // rows)
            queries = kept_ref[span, 0, :, columns(head)].reshape(count, HEAD_SIZE)
            grads = grad_ref[span, 0, :, columns(head)].reshape(count, HEAD_SIZE)
            chances = softmax_rows(queries, keys[:seen], starts_ref, micro, first)
            grad_prob = nt(grads, values[:seen])
            inner = jnp.sum(grad_prob * chances, axis=1, keepdims=True)
            grad_scores = (chances * (grad_prob - inner)).astype(BF16)
            grad_queries = nn(grad_scores, keys[:seen]) * SCALE
            place = slice(first, first + count)
            q_out[span, 0, :, columns(head)] = (
                turn(grad_queries, cosine_ref[place], sine_ref[place], -1.0)
                .astype(BF16)
                .reshape(count // rows, rows, HEAD_SIZE)
            )
            k_acc[:seen] += tn(grad_scores, queries)
            v_acc[:seen] += tn(chances.astype(BF16), grads)
    kv_out[:, 0, :, columns(0)] = (k_acc[...] * SCALE).reshape(parts, rows, HEAD_SIZE)
    kv_out[:, 0, :, columns(1)] = v_acc[...].reshape(parts, rows, HEAD_SIZE)


def per_micro(parts, rows, columns):
    return pl.BlockSpec((parts, 1, rows, columns), lambda micro: (0, micro, 0, 0))


def whole_table(length):
    return pl.BlockSpec((length, HEAD_SIZE), lambda micro: (0, 0))


def attend(qkv, starts, cosine, sine, heads):
    parts, _, rows, width = qkv.shape
    length = parts * rows
    return pl.pallas_call(
        functools.partial(attend_kernel, heads),
        grid=(MICRO,),
        out_shape=(
            jax.ShapeDtypeStruct(qkv.shape, BF16),
            jax.ShapeDtypeStruct((parts, MICRO, rows, heads * HEAD_SIZE), BF16),
        ),
        in_specs=[
            pl.BlockSpec(memory_space=pltpu.SMEM),
            per_micro(parts, rows, width),
            whole_table(length),
            whole_table(length),
        ],
        out_specs=(per_micro(parts, rows, width), per_micro(parts, rows, heads * HEAD_SIZE)),
        scratch_shapes=[
            pltpu.VMEM((length, HEAD_SIZE), BF16),
            pltpu.VMEM((length, HEAD_SIZE), BF16),
        ],
        compiler_params=pltpu.CompilerParams(vmem_limit_bytes=VMEM_LIMIT),
        cost_estimate=pl.CostEstimate(
            flops=MICRO * heads * 4 * length * length * HEAD_SIZE,
            bytes_accessed=8 * qkv.size,
            transcendentals=MICRO * heads * length * length,
        ),
        name="attend",
    )(starts, qkv, cosine, sine)


def attend_back(kept, grad_mixed, starts, cosine, sine, heads):
    parts, _, rows, width = kept.shape
    length = parts * rows
    return pl.pallas_call(
        functools.partial(attend_back_kernel, heads),
        grid=(MICRO,),
        out_shape=(
            jax.ShapeDtypeStruct(grad_mixed.shape, BF16),
            jax.ShapeDtypeStruct((parts, MICRO, rows, 2 * HEAD_SIZE), F32),
        ),
        in_specs=[
            pl.BlockSpec(memory_space=pltpu.SMEM),
            per_micro(parts, rows, width),
            per_micro(parts, rows, heads * HEAD_SIZE),
            whole_table(length),
            whole_table(length),
        ],
        out_specs=(
            per_micro(parts, rows, heads * HEAD_SIZE),
            per_micro(parts, rows, 2 * HEAD_SIZE),
        ),
        scratch_shapes=[
            pltpu.VMEM((length, HEAD_SIZE), F32),
            pltpu.VMEM((length, HEAD_SIZE), F32),
        ],
        compiler_params=pltpu.CompilerParams(vmem_limit_bytes=VMEM_LIMIT),
        cost_estimate=pl.CostEstimate(
            flops=MICRO * heads * 10 * length * length * HEAD_SIZE,
            bytes_accessed=8 * kept.size,
            transcendentals=MICRO * heads * length * length,
        ),
        name="attend_back",
    )(starts, kept, grad_mixed, cosine, sine)


def rotary_tables(length):
    half = HEAD_SIZE // 2
    frequency = jnp.power(ROTARY_BASE, -(jnp.arange(half).astype(F32) * (2.0 / HEAD_SIZE)))
    angles = jnp.arange(length).astype(F32)[:, None] * frequency[None, :]
    cosine, sine = jnp.cos(angles), jnp.sin(angles)
    return jnp.concatenate([cosine, cosine], axis=1), jnp.concatenate([-sine, sine], axis=1)


def inverse_rms(value):
    return lax.rsqrt(jnp.mean(value * value, axis=-1, keepdims=True) + EPSILON)


def norm_back(grad, value, inverse, gain):
    scaled = grad * gain
    return inverse * scaled - value * inverse**3 * jnp.mean(scaled * value, axis=-1, keepdims=True)


def shards(
    tokens,
    cotangent,
    piece_starts,
    attn_blocks,
    ffn_blocks,
    gains,
    left_stats,
    right_stats,
    left_root,
    right_root,
    owner_slot,
):
    fsdp, seq = lax.axis_size("fsdp"), lax.axis_size("seq")
    devices = fsdp * seq
    rows = attn_blocks.shape[0]
    count = tokens.shape[2]
    length = seq * count
    heads = QUERY_HEADS // seq
    sharing = max(1, seq // KEY_VALUE_HEADS)
    all_rows = MICRO * length
    feed = FF // seq
    starts = piece_starts[:, 0]
    cosine, sine = rotary_tables(length)

    def gather_tokens(value):
        return lax.all_gather(value, "seq", axis=0, tiled=False)

    def sum_tokens(term):
        term = term.astype(BF16).reshape(seq, MICRO, count, D)
        return lax.psum_scatter(term, "seq", scatter_dimension=0, tiled=False).astype(F32)

    q_cut = D_BLK * QUERY_HEADS * HEAD_SIZE // PRECOND_ORDER
    kv_blk = D_BLK * KEY_VALUE_HEADS * HEAD_SIZE // PRECOND_ORDER
    k_cut, v_cut = q_cut + kv_blk, q_cut + 2 * kv_blk
    attn_low, ffn_low = attn_blocks.astype(BF16), ffn_blocks.astype(BF16)

    def shared_parts(shard):
        return jnp.repeat(column_parts(shard, seq // sharing), sharing, axis=0)

    tokens_all = gather_tokens(tokens[:, 0])
    gain_all = lax.all_gather(gains.astype(BF16), BOTH, axis=1, tiled=True).astype(F32)
    qkv_w = gather_columns(
        jnp.concatenate(
            [
                column_parts(attn_low[:, :q_cut], seq),
                shared_parts(attn_low[:, q_cut:k_cut]),
                shared_parts(attn_low[:, k_cut:v_cut]),
            ],
            axis=-1,
        )
    )
    out_w = gather_rows(attn_low[:, v_cut:].reshape(rows, -1, D_BLK, PRECOND_ORDER))
    gu_cut = D_BLK * FF_BLK
    gu_w = gather_columns(
        jnp.concatenate(
            [
                column_parts(ffn_low[:, :gu_cut], seq),
                column_parts(ffn_low[:, gu_cut : 2 * gu_cut], seq),
            ],
            axis=-1,
        )
    )
    down_w = gather_rows(ffn_low[:, 2 * gu_cut :].reshape(rows, FF_BLK, D_BLK, PRECOND_ORDER))

    x_all = tokens_all.astype(F32)
    normed = (x_all * inverse_rms(x_all) * gain_all[0]).astype(BF16).reshape(all_rows, D)
    qkv = nn(normed, qkv_w).reshape(seq, MICRO, count, -1)
    kept, mixed = attend(qkv, starts, cosine, sine, heads)
    mixed = mixed.reshape(all_rows, heads * HEAD_SIZE)
    x = tokens[:, 0].astype(F32)
    inv_one = inverse_rms(x)
    hidden = x + sum_tokens(nn(mixed, out_w))
    inv_two = inverse_rms(hidden)
    normed_two = (hidden * inv_two * gain_all[1]).astype(BF16)
    normed_two_all = gather_tokens(normed_two).reshape(all_rows, D)
    gate_up = nn(normed_two_all, gu_w)
    gate, up = gate_up[:, :feed], gate_up[:, feed:]
    sigma = jax.nn.sigmoid(gate)
    inner = (gate * sigma * up).astype(BF16)
    cot_all = gather_tokens(cotangent[:, 0]).reshape(all_rows, D)

    grad_inner = nt(cot_all, down_w)
    grad_gu = jnp.concatenate(
        [
            (grad_inner * up * sigma * (1.0 + gate * (1.0 - sigma))).astype(BF16),
            (grad_inner * gate * sigma).astype(BF16),
        ],
        axis=1,
    )
    grad_norm_two = sum_tokens(nt(grad_gu, gu_w))
    block_out = (hidden + sum_tokens(nn(inner, down_w))).astype(BF16)
    gain_two = jnp.sum(grad_norm_two * hidden * inv_two, axis=(0, 1))
    grad_hidden = cotangent[:, 0].astype(F32) + norm_back(
        grad_norm_two, hidden, inv_two, gain_all[1]
    )
    grad_attn_all = gather_tokens(grad_hidden.astype(BF16)).reshape(all_rows, D)

    gu_rows = scatter_columns(tn(normed_two_all, grad_gu), rows)
    down_rows = scatter_rows(tn(inner, cot_all), rows)

    grad_mixed = nt(grad_attn_all, out_w).astype(BF16).reshape(seq, MICRO, count, -1)
    grad_q, grad_kv = attend_back(kept, grad_mixed, starts, cosine, sine, heads)
    if sharing > 1:
        groups = [[g * sharing + k for k in range(sharing)] for g in range(seq // sharing)]
        grad_kv = lax.psum(grad_kv, "seq", axis_index_groups=groups)
        grad_kv = jnp.where(lax.axis_index("seq") % sharing == 0, grad_kv, 0.0)
    grad_k, grad_v = grad_kv[..., :HEAD_SIZE], grad_kv[..., HEAD_SIZE:]
    half = HEAD_SIZE // 2
    swapped = jnp.concatenate([grad_k[..., half:], grad_k[..., :half]], axis=-1)
    table = (seq, 1, count, HEAD_SIZE)
    grad_k = grad_k * cosine.reshape(table) - swapped * sine.reshape(table)
    grad_qkv = jnp.concatenate([grad_q, grad_k.astype(BF16), grad_v.astype(BF16)], axis=-1)
    grad_qkv = grad_qkv.reshape(all_rows, -1)
    grad_norm_one = sum_tokens(nt(grad_qkv, qkv_w))
    gain_one = jnp.sum(grad_norm_one * x * inv_one, axis=(0, 1))
    input_grad = (grad_hidden + norm_back(grad_norm_one, x, inv_one, gain_all[0])).astype(BF16)
    gain_grad = lax.psum_scatter(
        jnp.stack([gain_one, gain_two]), BOTH, scatter_dimension=1, tiled=True
    )
    qkv_rows = scatter_columns(tn(normed, grad_qkv), rows)
    out_rows = scatter_rows(tn(mixed, grad_attn_all), rows)

    def column_blocks(part):
        return part.transpose(2, 0, 1, 3).reshape(rows, -1, PRECOND_ORDER)

    def row_blocks(part):
        return part.transpose(1, 0, 2).reshape(rows, -1, PRECOND_ORDER)

    def shared_blocks(part):
        return column_blocks(part[:, ::sharing])

    q_width = heads * HEAD_SIZE
    attn_grad = jnp.concatenate(
        [
            column_blocks(qkv_rows[..., :q_width]),
            shared_blocks(qkv_rows[..., q_width : q_width + HEAD_SIZE]),
            shared_blocks(qkv_rows[..., q_width + HEAD_SIZE :]),
            row_blocks(out_rows),
        ],
        axis=1,
    )
    ffn_grad = jnp.concatenate(
        [
            column_blocks(gu_rows[..., :feed]),
            column_blocks(gu_rows[..., feed:]),
            row_blocks(down_rows),
        ],
        axis=1,
    )

    grad_all = jnp.concatenate([attn_grad, ffn_grad], axis=1)
    slots = left_stats.shape[0]
    blocks = grad_all.shape[1]
    slot_table = jnp.arange(slots)[:, None] + jnp.arange(devices)[None, :] * slots
    slot_match = owner_slot[None, None, :] == slot_table[:, :, None]
    slot_block = jnp.sum(jnp.where(slot_match, jnp.arange(blocks)[None, None, :], 0), axis=-1)
    filled = jnp.any(slot_match, axis=-1)
    by_block = jnp.transpose(grad_all, (1, 0, 2))
    outgoing = jnp.where(filled[:, :, None, None], by_block[slot_block], 0.0).astype(BF16)
    held = lax.all_to_all(outgoing, BOTH, split_axis=1, concat_axis=1, tiled=True)
    held = held.reshape(slots, PRECOND_ORDER, PRECOND_ORDER)
    own_slots = lax.axis_index(BOTH) * slots + jnp.arange(slots)
    owned = jnp.any(owner_slot[None, :] == own_slots[:, None], axis=-1)[:, None, None]

    def batched(a, b, a_dim, b_dim):
        return lax.dot_general(
            a, b, (((a_dim,), (b_dim,)), ((0,), (0,))), preferred_element_type=F32
        )

    step = batched(left_root.astype(BF16), held, 2, 1)
    step = batched(step.astype(BF16), right_root.astype(BF16), 2, 1).astype(BF16)
    returned = lax.all_to_all(
        step.reshape(slots, devices, rows, PRECOND_ORDER),
        BOTH,
        split_axis=1,
        concat_axis=1,
        tiled=True,
    )
    normalizer = 1.0 * MICRO * fsdp * length * PRECOND_ORDER
    gram_left = batched(held, held, 2, 2) / normalizer
    gram_right = batched(held, held, 1, 1) / normalizer
    new_left = jnp.where(
        owned, STAT_DECAY * left_stats + (1.0 - STAT_DECAY) * gram_left, left_stats
    )
    new_right = jnp.where(
        owned, STAT_DECAY * right_stats + (1.0 - STAT_DECAY) * gram_right, right_stats
    )
    flat = jnp.transpose(returned, (1, 0, 2, 3)).reshape(devices * slots, rows, PRECOND_ORDER)
    update = jnp.transpose(flat[owner_slot], (1, 0, 2)).astype(F32)
    attn_count = attn_blocks.shape[1]
    return (
        block_out[:, None],
        input_grad[:, None],
        attn_grad.astype(F32),
        ffn_grad.astype(F32),
        gain_grad,
        attn_blocks - STEP_RATE * update[:, :attn_count],
        ffn_blocks - STEP_RATE * update[:, attn_count:],
        gains - GAIN_RATE * gain_grad,
        new_left,
        new_right,
    )


def solution(mesh):
    by_token = P(None, "fsdp", "seq", None)
    by_row = P(BOTH, None, None)
    by_gain = P(None, BOTH)
    return jax.shard_map(
        shards,
        mesh=mesh,
        in_specs=(
            by_token,
            by_token,
            P(None, "fsdp", None),
            by_row,
            by_row,
            by_gain,
            by_row,
            by_row,
            by_row,
            by_row,
            P(),
        ),
        out_specs=(
            by_token,
            by_token,
            by_row,
            by_row,
            by_gain,
            by_row,
            by_row,
            by_gain,
            by_row,
            by_row,
        ),
        check_vma=False,
    )
```

```python
import functools

import jax
import jax.numpy as jnp
from jax import lax
from jax.experimental import pallas as pl
from jax.experimental.pallas import tpu as pltpu
from jax.sharding import PartitionSpec as P

D = 2048
QUERY_HEADS = 16
KEY_VALUE_HEADS = 8
HEAD_SIZE = 128
FF = 8192
PRECOND_ORDER = 1024
MICRO = 2
PIECE = 256

EPSILON = 1e-06
ROTARY_BASE = 1000000.0
STAT_DECAY = 0.5
STEP_RATE = 1.0
GAIN_RATE = 0.001

F32 = jnp.float32
BF16 = jnp.bfloat16
BOTH = ("fsdp", "seq")
SCALE = HEAD_SIZE ** (-0.5)
QUERY_ROWS = 256
D_BLK = D // PRECOND_ORDER
FF_BLK = FF // PRECOND_ORDER
VMEM_LIMIT = 56 * 1024 * 1024
TILE = 512
LINE_CHIPS = 4
MESH = pl.DeviceIdType.MESH


def dot(a, b, contract):
    return lax.dot_general(a, b, (contract, ((), ())), preferred_element_type=F32)


def nn(a, b):
    return dot(a, b, ((1,), (0,)))


def nt(a, b):
    return dot(a, b, ((1,), (1,)))


def tn(a, b):
    return dot(a, b, ((0,), (0,)))


def swap_seq(array, axis):
    return lax.all_to_all(array, "seq", split_axis=axis, concat_axis=axis, tiled=True)


def sum_fsdp(array):
    arrived = lax.all_to_all(array, "fsdp", split_axis=0, concat_axis=0, tiled=True)
    return jnp.sum(arrived.astype(F32), axis=0).astype(BF16)


def column_parts(shard, parts):
    rows = shard.shape[0]
    columns = shard.shape[1] // D_BLK * PRECOND_ORDER // parts
    return shard.reshape(rows, D_BLK, parts, columns).transpose(2, 1, 0, 3)


def gather_columns(parts):
    swapped = swap_seq(parts, 0)
    whole = lax.all_gather(swapped, "fsdp", axis=0, tiled=False)
    return whole.transpose(2, 0, 1, 3, 4).reshape(D, parts.shape[-1])


def scatter_columns(term, rows):
    seq, fsdp = lax.axis_size("seq"), lax.axis_size("fsdp")
    shaped = term.astype(BF16).reshape(D_BLK, fsdp, seq, rows, term.shape[1]).transpose(1, 0, 2, 3, 4)
    return swap_seq(sum_fsdp(shaped), 1)


def gather_rows(shard):
    seq, fsdp = lax.axis_size("seq"), lax.axis_size("fsdp")
    rows, groups = shard.shape[:2]
    by_group = shard.reshape(rows, groups, D).transpose(1, 0, 2)
    if groups == seq:
        swapped = swap_seq(by_group, 0)
        whole = lax.all_gather(swapped, "fsdp", axis=0, tiled=False)
        return whole.reshape(PRECOND_ORDER, D)
    whole = lax.all_gather(by_group, "fsdp", axis=1, tiled=False)
    pieces = whole.reshape(seq, groups * fsdp // seq, rows, D)
    swapped = swap_seq(pieces, 0)
    return swapped.transpose(1, 0, 2, 3).reshape(groups * PRECOND_ORDER // seq, D)


def scatter_rows(term, rows):
    seq, fsdp = lax.axis_size("seq"), lax.axis_size("fsdp")
    groups = term.shape[0] * seq // PRECOND_ORDER
    term = term.astype(BF16)
    if groups == seq:
        return swap_seq(sum_fsdp(term.reshape(fsdp, seq, rows, D)), 0)
    pieces = term.reshape(groups * fsdp // seq, seq, rows, D).transpose(1, 0, 2, 3)
    swapped = swap_seq(pieces, 0).reshape(groups, fsdp, rows, D).transpose(1, 0, 2, 3)
    return sum_fsdp(swapped)


def turn(value, cosine, sine, sign):
    return value * cosine + sign * (pltpu.roll(value, HEAD_SIZE // 2, 1) * sine)


def piece_index(starts_ref, micro, position, outside):
    index = jnp.full(position.shape, outside, jnp.int32)
    for piece in range(starts_ref.shape[1]):
        start = starts_ref[micro, piece]
        index = jnp.where((position >= start) & (position < start + PIECE), piece, index)
    return index


def softmax_rows(queries, keys, starts_ref, micro, first):
    rows, length = queries.shape[0], keys.shape[0]
    query_pos = first + lax.broadcasted_iota(jnp.int32, (rows, 1), 0)
    key_pos = lax.broadcasted_iota(jnp.int32, (1, length), 1)
    same = piece_index(starts_ref, micro, query_pos, -1) == piece_index(
        starts_ref, micro, key_pos, -2
    )
    scores = jnp.where((key_pos <= query_pos) | same, nt(queries, keys) * SCALE, -1e30)
    exponent = jnp.exp(scores - jnp.max(scores, axis=1, keepdims=True))
    return exponent / jnp.sum(exponent, axis=1, keepdims=True)


def query_blocks(length):
    rows = min(QUERY_ROWS, length)
    for first in range(0, length, rows):
        yield first, rows, min(length, first + rows + PIECE)


def attend_kernel(heads, starts_ref, qkv_ref, cosine_ref, sine_ref, kept_ref, mixed_ref, k_ref, v_ref):
    micro = pl.program_id(0)
    parts, _, rows, _ = qkv_ref.shape
    length = parts * rows
    cosine, sine = cosine_ref[...], sine_ref[...]

    def columns(head):
        return pl.ds(head * HEAD_SIZE, HEAD_SIZE)

    def turned(head):
        value = qkv_ref[:, 0, :, columns(head)].reshape(length, HEAD_SIZE)
        return turn(value, cosine, sine, 1.0).astype(BF16)

    def keep(head, value):
        kept_ref[:, 0, :, columns(head)] = value.reshape(parts, rows, HEAD_SIZE)

    k_ref[...] = turned(heads)
    v_ref[...] = qkv_ref[:, 0, :, columns(heads + 1)].reshape(length, HEAD_SIZE).astype(BF16)
    keep(heads, k_ref[...])
    keep(heads + 1, v_ref[...])
    for head in range(heads):
        queries = turned(head)
        keep(head, queries)
        for first, count, seen in query_blocks(length):
            chances = softmax_rows(
                queries[first : first + count], k_ref[:seen], starts_ref, micro, first
            )
            mixed = nn(chances.astype(BF16), v_ref[:seen]).astype(BF16)
            mixed_ref[first // rows : (first + count) // rows, 0, :, columns(head)] = mixed.reshape(
                count // rows, rows, HEAD_SIZE
            )


def attend_back_kernel(
    heads, starts_ref, kept_ref, grad_ref, cosine_ref, sine_ref, q_out, kv_out, k_acc, v_acc
):
    micro = pl.program_id(0)
    parts, _, rows, _ = kept_ref.shape
    length = parts * rows

    def columns(head):
        return pl.ds(head * HEAD_SIZE, HEAD_SIZE)

    keys = kept_ref[:, 0, :, columns(heads)].reshape(length, HEAD_SIZE)
    values = kept_ref[:, 0, :, columns(heads + 1)].reshape(length, HEAD_SIZE)
    k_acc[...] = jnp.zeros_like(k_acc)
    v_acc[...] = jnp.zeros_like(v_acc)
    for head in range(heads):
        for first, count, seen in query_blocks(length):
            span = slice(first // rows, (first + count) // rows)
            queries = kept_ref[span, 0, :, columns(head)].reshape(count, HEAD_SIZE)
            grads = grad_ref[span, 0, :, columns(head)].reshape(count, HEAD_SIZE)
            chances = softmax_rows(queries, keys[:seen], starts_ref, micro, first)
            grad_prob = nt(grads, values[:seen])
            inner = jnp.sum(grad_prob * chances, axis=1, keepdims=True)
            grad_scores = (chances * (grad_prob - inner)).astype(BF16)
            grad_queries = nn(grad_scores, keys[:seen]) * SCALE
            place = slice(first, first + count)
            q_out[span, 0, :, columns(head)] = (
                turn(grad_queries, cosine_ref[place], sine_ref[place], -1.0)
                .astype(BF16)
                .reshape(count // rows, rows, HEAD_SIZE)
            )
            k_acc[:seen] += tn(grad_scores, queries)
            v_acc[:seen] += tn(chances.astype(BF16), grads)
    kv_out[:, 0, :, columns(0)] = (k_acc[...] * SCALE).reshape(parts, rows, HEAD_SIZE)
    kv_out[:, 0, :, columns(1)] = v_acc[...].reshape(parts, rows, HEAD_SIZE)


def per_micro(parts, rows, columns):
    return pl.BlockSpec((parts, 1, rows, columns), lambda micro: (0, micro, 0, 0))


def whole_table(length):
    return pl.BlockSpec((length, HEAD_SIZE), lambda micro: (0, 0))


def attend(qkv, starts, cosine, sine, heads):
    parts, _, rows, width = qkv.shape
    length = parts * rows
    return pl.pallas_call(
        functools.partial(attend_kernel, heads),
        grid=(MICRO,),
        out_shape=(
            jax.ShapeDtypeStruct(qkv.shape, BF16),
            jax.ShapeDtypeStruct((parts, MICRO, rows, heads * HEAD_SIZE), BF16),
        ),
        in_specs=[
            pl.BlockSpec(memory_space=pltpu.SMEM),
            per_micro(parts, rows, width),
            whole_table(length),
            whole_table(length),
        ],
        out_specs=(per_micro(parts, rows, width), per_micro(parts, rows, heads * HEAD_SIZE)),
        scratch_shapes=[
            pltpu.VMEM((length, HEAD_SIZE), BF16),
            pltpu.VMEM((length, HEAD_SIZE), BF16),
        ],
        compiler_params=pltpu.CompilerParams(vmem_limit_bytes=VMEM_LIMIT),
        cost_estimate=pl.CostEstimate(
            flops=MICRO * heads * 4 * length * length * HEAD_SIZE,
            bytes_accessed=8 * qkv.size,
            transcendentals=MICRO * heads * length * length,
        ),
        name="attend",
    )(starts, qkv, cosine, sine)


def attend_back(kept, grad_mixed, starts, cosine, sine, heads):
    parts, _, rows, width = kept.shape
    length = parts * rows
    return pl.pallas_call(
        functools.partial(attend_back_kernel, heads),
        grid=(MICRO,),
        out_shape=(
            jax.ShapeDtypeStruct(grad_mixed.shape, BF16),
            jax.ShapeDtypeStruct((parts, MICRO, rows, 2 * HEAD_SIZE), F32),
        ),
        in_specs=[
            pl.BlockSpec(memory_space=pltpu.SMEM),
            per_micro(parts, rows, width),
            per_micro(parts, rows, heads * HEAD_SIZE),
            whole_table(length),
            whole_table(length),
        ],
        out_specs=(
            per_micro(parts, rows, heads * HEAD_SIZE),
            per_micro(parts, rows, 2 * HEAD_SIZE),
        ),
        scratch_shapes=[
            pltpu.VMEM((length, HEAD_SIZE), F32),
            pltpu.VMEM((length, HEAD_SIZE), F32),
        ],
        compiler_params=pltpu.CompilerParams(vmem_limit_bytes=VMEM_LIMIT),
        cost_estimate=pl.CostEstimate(
            flops=MICRO * heads * 10 * length * length * HEAD_SIZE,
            bytes_accessed=8 * kept.size,
            transcendentals=MICRO * heads * length * length,
        ),
        name="attend_back",
    )(starts, kept, grad_mixed, cosine, sine)


def rotary_tables(length):
    half = HEAD_SIZE // 2
    frequency = jnp.power(ROTARY_BASE, -(jnp.arange(half).astype(F32) * (2.0 / HEAD_SIZE)))
    angles = jnp.arange(length).astype(F32)[:, None] * frequency[None, :]
    cosine, sine = jnp.cos(angles), jnp.sin(angles)
    return jnp.concatenate([cosine, cosine], axis=1), jnp.concatenate([-sine, sine], axis=1)


class Place:
    def __init__(self, seq):
        self.count = seq // 2
        self.me = lax.axis_index("seq")
        self.spot = lax.div(self.me, 2)
        self.core = lax.rem(self.me, 2)
        self.sibling = self.me + 1 - 2 * self.core
        first = jnp.where(2 * self.spot < self.count, 1, -1)
        self.ways = [Way(self, number, sign) for number, sign in enumerate((first, -first))]

    def greet(self):
        barrier = pltpu.get_barrier_semaphore()

        def signal(device):
            pl.semaphore_signal(barrier, inc=1, device_id={"seq": device}, device_id_type=MESH)

        signal(self.sibling)
        for sign, there in ((-1, self.spot > 0), (1, self.spot < self.count - 1)):

            @pl.when(there)
            def _():
                signal(self.me + 2 * sign)

        ends = (self.spot > 0).astype(jnp.int32) + (self.spot < self.count - 1).astype(jnp.int32)
        pl.semaphore_wait(barrier, 1 + ends)


class Way:
    def __init__(self, place, number, sign):
        self.number = number
        self.lane = lax.div(1 - sign, 2)
        self.last = place.count - 1
        self.sign = sign
        self.behind = jnp.where(sign == 1, place.spot, self.last - place.spot)
        self.ahead = place.me + 2 * sign

    def spot(self, mirrored):
        return jnp.where(self.sign == 1, mirrored, self.last - mirrored)


class Gather:
    def __init__(self, place, own, chunks, kept, sems):
        self.place, self.own, self.chunks, self.kept = place, own, chunks, kept
        self.send, self.recv, self.give, self.take, self.keep_sem, self.own_sem = sems
        self.steps = place.count - 1

    def line(self, way, step):
        index = 2 * way.spot(way.behind - step) + self.place.core
        return pltpu.make_async_remote_copy(
            src_ref=self.own if step == 0 else self.chunks.at[index],
            dst_ref=self.chunks.at[index],
            send_sem=self.send.at[way.lane, step],
            recv_sem=self.recv.at[way.lane, step],
            device_id={"seq": way.ahead},
            device_id_type=MESH,
        )

    def arriving(self, way, step):
        return 2 * way.spot(way.behind - 1 - step) + self.place.core

    def arrival(self, way, step):
        index = self.arriving(way, step)
        return pltpu.make_async_remote_copy(
            src_ref=self.chunks.at[index],
            dst_ref=self.chunks.at[index],
            send_sem=self.send.at[way.lane, step],
            recv_sem=self.recv.at[way.lane, step],
            device_id={"seq": way.ahead},
            device_id_type=MESH,
        )

    def pair(self, index, event):
        return pltpu.make_async_remote_copy(
            src_ref=self.own if event == 0 else self.chunks.at[index],
            dst_ref=self.chunks.at[index],
            send_sem=self.give.at[event],
            recv_sem=self.take.at[event],
            device_id={"seq": self.place.sibling},
            device_id_type=MESH,
        )

    def keep(self, index):
        return pltpu.make_async_copy(
            self.chunks.at[index], self.kept.at[index], self.keep_sem.at[index]
        )

    def other(self, index):
        return index + 1 - 2 * self.place.core

    def event(self, way, step):
        return 1 + way.number * self.steps + step

    def start(self):
        me = self.place.me
        mine = pltpu.make_async_copy(self.own, self.chunks.at[me], self.own_sem)
        mine.start()
        for way in self.place.ways:

            @pl.when(way.behind < self.steps)
            def _():
                self.line(way, 0).start()

        self.pair(me, 0).start()
        mine.wait()
        self.keep(me).start()

    def visit_own(self, visit):
        me = self.place.me
        visit(me)
        self.pair(self.other(me), 0).wait_recv()
        self.keep(self.other(me)).start()
        visit(self.other(me))

    def pass_on(self, way, step):
        @pl.when(way.behind - 1 - step >= 0)
        def _():
            index = self.arriving(way, step)
            self.arrival(way, step).wait_recv()
            if step + 1 < self.steps:

                @pl.when(way.behind < self.steps)
                def _():
                    self.line(way, step + 1).start()

            self.pair(index, self.event(way, step)).start()
            self.keep(index).start()

    def visit_step(self, way, step, visit):
        @pl.when(way.behind - 1 - step >= 0)
        def _():
            index = self.arriving(way, step)
            visit(index)
            self.pair(self.other(index), self.event(way, step)).wait_recv()
            self.keep(self.other(index)).start()
            visit(self.other(index))

    def finish(self):
        me = self.place.me
        self.pair(me, 0).wait_send()
        self.keep(me).wait()
        self.keep(self.other(me)).wait()
        for way in self.place.ways:
            for step in range(self.steps):

                @pl.when((way.behind < self.steps) & (way.behind - step >= 0))
                def _():
                    self.line(way, step).wait_send()

                @pl.when(way.behind - 1 - step >= 0)
                def _():
                    index = self.arriving(way, step)
                    self.pair(index, self.event(way, step)).wait_send()
                    self.keep(index).wait()
                    self.keep(self.other(index)).wait()


class Scatter:
    def __init__(self, place, term, buffers, sems):
        self.place, self.term = place, term
        self.stage, self.lent, self.slots, self.work = buffers
        self.send, self.recv, self.give, self.take = sems
        self.steps = place.count - 1
        self.tiles = D // TILE

    def for_tiles(self, body):
        @pl.loop(0, self.tiles)
        def _(number):
            body(pl.ds(pl.multiple_of(number * TILE, TILE), TILE))

    def lend_copy(self, spot):
        return pltpu.make_async_remote_copy(
            src_ref=self.stage.at[spot],
            dst_ref=self.lent.at[spot],
            send_sem=self.give.at[spot],
            recv_sem=self.take.at[spot],
            device_id={"seq": self.place.sibling},
            device_id_type=MESH,
        )

    def lend(self, spot):
        index = 2 * spot + 1 - self.place.core

        def body(columns):
            self.stage[spot, :, columns] = self.term(index, columns).astype(BF16)

        self.for_tiles(body)
        self.lend_copy(spot).start()

    def own_term(self, spot):
        index = 2 * spot + self.place.core
        self.lend_copy(spot).wait_recv()

        def body(columns):
            self.work[:, columns] = self.term(index, columns) + self.lent[spot, :, columns].astype(F32)

        self.for_tiles(body)

    def line(self, way, step):
        return pltpu.make_async_remote_copy(
            src_ref=self.slots.at[way.lane, step],
            dst_ref=self.slots.at[way.lane, step],
            send_sem=self.send.at[way.lane, step],
            recv_sem=self.recv.at[way.lane, step],
            device_id={"seq": way.ahead},
            device_id_type=MESH,
        )

    def sends(self, way, step):
        return step < self.steps - way.behind

    def lend_step(self, way, step):
        @pl.when(self.sends(way, step))
        def _():
            self.lend(way.spot(self.steps - step))

    def add_step(self, way, step):
        @pl.when(self.sends(way, step))
        def _():
            self.own_term(way.spot(self.steps - step))

            @pl.when(way.behind > 0)
            def _():
                self.line(way, step).wait_recv()

                def body(columns):
                    slot = self.slots[way.lane, step, :, columns].astype(F32)
                    self.slots[way.lane, step, :, columns] = (self.work[:, columns] + slot).astype(BF16)

                self.for_tiles(body)

            @pl.when(way.behind == 0)
            def _():
                def body(columns):
                    self.slots[way.lane, step, :, columns] = self.work[:, columns].astype(BF16)

                self.for_tiles(body)

            self.line(way, step).start()

    def own_sum(self, total):
        self.own_term(self.place.spot)
        total[...] = self.work[...]
        for way in self.place.ways:

            @pl.when(way.behind > 0)
            def _():
                step = self.steps - way.behind
                self.line(way, step).wait_recv()

                def body(columns):
                    total[:, columns] += self.slots[way.lane, step, :, columns].astype(F32)

                self.for_tiles(body)

    def finish(self):
        for spot in range(self.place.count):
            self.lend_copy(spot).wait_send()
        for way in self.place.ways:
            for step in range(self.steps):

                @pl.when(self.sends(way, step))
                def _():
                    self.line(way, step).wait_send()


def exchange_kernel(seq, gathers, scatters, transposed, visit, extra_in, extra_out, *refs):
    refs = list(refs)

    def take(number):
        taken, refs[:] = refs[:number], refs[number:]
        return taken

    own = take(gathers)
    terms = take(2 * scatters)
    more_in = take(extra_in)
    kept = take(gathers)
    total = take(scatters)
    more_out = take(extra_out)
    place = Place(seq)
    gather = scatter = None
    if gathers:
        chunks = take(1)[0]
        gather = Gather(place, own[0], chunks, kept[0], take(6))
    if scatters:
        a_ref, b_ref = terms

        def term(index, columns):
            if transposed:
                return nt(a_ref[index], b_ref[columns, :])
            return nn(a_ref[index], b_ref[:, columns])

        scatter = Scatter(place, term, take(4), take(4))

    def see(index):
        if visit is not None:
            visit(index, chunks, more_in, more_out)

    place.greet()
    if gather:
        gather.start()
    if scatter:
        for way in place.ways:
            scatter.lend_step(way, 0)
    if gather and not scatter:
        gather.visit_own(see)
    for step in range(place.count - 1):
        near, far = place.ways
        if scatter:
            scatter.add_step(near, step)
        if gather:
            gather.pass_on(near, step)
            gather.pass_on(far, step)
        if scatter:
            if step + 1 < place.count - 1:
                for way in place.ways:
                    scatter.lend_step(way, step + 1)
            else:
                scatter.lend(place.spot)
            scatter.add_step(far, step)
        if gather:
            if scatter and step == 0:
                gather.visit_own(see)
            gather.visit_step(near, step, see)
            gather.visit_step(far, step, see)
    if scatter:
        scatter.own_sum(total[0])
        scatter.finish()
    if gather:
        gather.finish()


def exchange(
    number,
    seq,
    own=None,
    terms=None,
    transposed=False,
    visit=None,
    extra_in=(),
    extra_out=(),
    flops=0,
):
    gathers, scatters = int(own is not None), int(terms is not None)
    chips = seq // 2
    rows = own.shape[0] if gathers else terms[0].shape[1]
    vmem = pl.BlockSpec(memory_space=pltpu.VMEM)
    operands, outs, out_specs, scratch = [], [], [], []
    dma = pltpu.SemaphoreType.DMA
    if gathers:
        operands.append(own)
        outs.append(jax.ShapeDtypeStruct((seq, rows, D), BF16))
        out_specs.append(pl.BlockSpec(memory_space=pl.ANY))
        scratch += [
            pltpu.VMEM((seq, rows, D), BF16),
            dma((2, chips - 1)),
            dma((2, chips - 1)),
            dma((2 * chips - 1,)),
            dma((2 * chips - 1,)),
            dma((seq,)),
            dma,
        ]
    if scatters:
        operands += list(terms)
        outs.append(jax.ShapeDtypeStruct((rows, D), F32))
        out_specs.append(vmem)
        scratch += [
            pltpu.VMEM((chips, rows, D), BF16),
            pltpu.VMEM((chips, rows, D), BF16),
            pltpu.VMEM((2, chips - 1, rows, D), BF16),
            pltpu.VMEM((rows, D), F32),
            dma((2, chips - 1)),
            dma((2, chips - 1)),
            dma((chips,)),
            dma((chips,)),
        ]
    operands += list(extra_in)
    outs += list(extra_out)
    out_specs += [vmem] * len(extra_out)
    return pl.pallas_call(
        functools.partial(
            exchange_kernel,
            seq,
            gathers,
            scatters,
            transposed,
            visit,
            len(extra_in),
            len(extra_out),
        ),
        out_shape=tuple(outs),
        in_specs=[vmem] * len(operands),
        out_specs=tuple(out_specs),
        scratch_shapes=scratch,
        compiler_params=pltpu.CompilerParams(
            collective_id=number, has_side_effects=True, vmem_limit_bytes=VMEM_LIMIT
        ),
        cost_estimate=pl.CostEstimate(
            flops=flops, bytes_accessed=250 * 1000 * 1000, transcendentals=0
        ),
        name="exchange_" + str(number),
    )(*operands)


def feed_visit(index, chunks, more_in, more_out):
    cot_ref, gu_ref, down_ref = more_in
    inner_ref, grad_ref = more_out
    feed = down_ref.shape[0]
    width = min(256, feed)

    @pl.loop(0, feed // width)
    def _(number):
        start = pl.multiple_of(number * width, width)
        gate_columns = pl.ds(start, width)
        up_columns = pl.ds(pl.multiple_of(feed + start, width), width)
        rows = chunks[index]
        gate = nn(rows, gu_ref[:, gate_columns])
        up = nn(rows, gu_ref[:, up_columns])
        grad_inner = nt(cot_ref[index], down_ref[gate_columns, :])
        sigma = jax.nn.sigmoid(gate)
        inner_ref[index, :, gate_columns] = (gate * sigma * up).astype(BF16)
        grad_ref[index, :, gate_columns] = (
            grad_inner * up * sigma * (1.0 + gate * (1.0 - sigma))
        ).astype(BF16)
        grad_ref[index, :, up_columns] = (grad_inner * gate * sigma).astype(BF16)


def mixed_visit(index, chunks, more_in, more_out):
    more_out[0][index] = nt(chunks[index], more_in[0][...]).astype(BF16)


def inverse_rms(value):
    return lax.rsqrt(jnp.mean(value * value, axis=-1, keepdims=True) + EPSILON)


def norm_back(grad, value, inverse, gain):
    scaled = grad * gain
    return inverse * scaled - value * inverse**3 * jnp.mean(scaled * value, axis=-1, keepdims=True)


def shards(
    tokens,
    cotangent,
    piece_starts,
    attn_blocks,
    ffn_blocks,
    gains,
    left_stats,
    right_stats,
    left_root,
    right_root,
    owner_slot,
):
    fsdp, seq = lax.axis_size("fsdp"), lax.axis_size("seq")
    devices = fsdp * seq
    rows = attn_blocks.shape[0]
    count = tokens.shape[2]
    length = seq * count
    heads = QUERY_HEADS // seq
    sharing = max(1, seq // KEY_VALUE_HEADS)
    all_rows = MICRO * length
    feed = FF // seq
    starts = piece_starts[:, 0]
    cosine, sine = rotary_tables(length)

    def gather_tokens(value):
        return lax.all_gather(value, "seq", axis=0, tiled=False)

    def sum_tokens(term):
        term = term.astype(BF16).reshape(seq, MICRO, count, D)
        return lax.psum_scatter(term, "seq", scatter_dimension=0, tiled=False).astype(F32)

    q_cut = D_BLK * QUERY_HEADS * HEAD_SIZE // PRECOND_ORDER
    kv_blk = D_BLK * KEY_VALUE_HEADS * HEAD_SIZE // PRECOND_ORDER
    k_cut, v_cut = q_cut + kv_blk, q_cut + 2 * kv_blk
    attn_low, ffn_low = attn_blocks.astype(BF16), ffn_blocks.astype(BF16)

    def shared_parts(shard):
        return jnp.repeat(column_parts(shard, seq // sharing), sharing, axis=0)

    tokens_all = gather_tokens(tokens[:, 0])
    gain_all = lax.all_to_all(
        jnp.broadcast_to(gains.astype(BF16)[None], (devices,) + gains.shape),
        BOTH,
        split_axis=0,
        concat_axis=0,
        tiled=True,
    )
    gain_all = gain_all.transpose(1, 0, 2).reshape(2, D).astype(F32)
    qkv_w = gather_columns(
        jnp.concatenate(
            [
                column_parts(attn_low[:, :q_cut], seq),
                shared_parts(attn_low[:, q_cut:k_cut]),
                shared_parts(attn_low[:, k_cut:v_cut]),
            ],
            axis=-1,
        )
    )
    out_w = gather_rows(attn_low[:, v_cut:].reshape(rows, -1, D_BLK, PRECOND_ORDER))
    gu_cut = D_BLK * FF_BLK
    gu_w = gather_columns(
        jnp.concatenate(
            [
                column_parts(ffn_low[:, :gu_cut], seq),
                column_parts(ffn_low[:, gu_cut : 2 * gu_cut], seq),
            ],
            axis=-1,
        )
    )
    down_w = gather_rows(ffn_low[:, 2 * gu_cut :].reshape(rows, FF_BLK, D_BLK, PRECOND_ORDER))

    chunk_rows = MICRO * count
    lined = seq == 2 * LINE_CHIPS

    def chunked(value):
        return value.reshape(seq, chunk_rows, -1)

    x_all = tokens_all.astype(F32)
    normed = (x_all * inverse_rms(x_all) * gain_all[0]).astype(BF16).reshape(all_rows, D)
    qkv = nn(normed, qkv_w).reshape(seq, MICRO, count, -1)
    kept, mixed = attend(qkv, starts, cosine, sine, heads)
    mixed = mixed.reshape(all_rows, heads * HEAD_SIZE)
    x = tokens[:, 0].astype(F32)
    inv_one = inverse_rms(x)
    cot_own = cotangent[:, 0].reshape(chunk_rows, D)
    if lined:
        cot_all, summed = exchange(0, seq, own=cot_own, terms=(chunked(mixed), out_w))
        cot_all, summed = cot_all.reshape(all_rows, D), summed.reshape(MICRO, count, D)
    else:
        cot_all = gather_tokens(cotangent[:, 0]).reshape(all_rows, D)
        summed = sum_tokens(nn(mixed, out_w))
    hidden = x + summed
    inv_two = inverse_rms(hidden)
    normed_two = (hidden * inv_two * gain_all[1]).astype(BF16)
    if lined:
        normed_two_all, inner, grad_gu = exchange(
            1,
            seq,
            own=normed_two.reshape(chunk_rows, D),
            visit=feed_visit,
            extra_in=(chunked(cot_all), gu_w, down_w),
            extra_out=(
                jax.ShapeDtypeStruct((seq, chunk_rows, feed), BF16),
                jax.ShapeDtypeStruct((seq, chunk_rows, 2 * feed), BF16),
            ),
        )
        normed_two_all = normed_two_all.reshape(all_rows, D)
        inner, grad_gu = inner.reshape(all_rows, feed), grad_gu.reshape(all_rows, 2 * feed)
    else:
        normed_two_all = gather_tokens(normed_two).reshape(all_rows, D)
        gate_up = nn(normed_two_all, gu_w)
        gate, up = gate_up[:, :feed], gate_up[:, feed:]
        sigma = jax.nn.sigmoid(gate)
        inner = (gate * sigma * up).astype(BF16)
        grad_inner = nt(cot_all, down_w)
        grad_gu = jnp.concatenate(
            [
                (grad_inner * up * sigma * (1.0 + gate * (1.0 - sigma))).astype(BF16),
                (grad_inner * gate * sigma).astype(BF16),
            ],
            axis=1,
        )

    gu_term = tn(normed_two_all, grad_gu).astype(BF16)
    down_term = tn(inner, cot_all).astype(BF16)
    grad_gu, gu_term, down_term = lax.optimization_barrier((grad_gu, gu_term, down_term))
    if lined:
        (grad_norm_two,) = exchange(2, seq, terms=(chunked(grad_gu), gu_w), transposed=True)
        grad_norm_two = grad_norm_two.reshape(MICRO, count, D)
    else:
        grad_norm_two = sum_tokens(nt(grad_gu, gu_w))
    gain_two = jnp.sum(grad_norm_two * hidden * inv_two, axis=(0, 1))
    grad_hidden = cotangent[:, 0].astype(F32) + norm_back(
        grad_norm_two, hidden, inv_two, gain_all[1]
    )
    grad_attn = grad_hidden.astype(BF16)
    if lined:
        grad_attn_all, summed, grad_mixed = exchange(
            3,
            seq,
            own=grad_attn.reshape(chunk_rows, D),
            terms=(chunked(inner), down_w),
            visit=mixed_visit,
            extra_in=(out_w,),
            extra_out=(jax.ShapeDtypeStruct((seq, chunk_rows, heads * HEAD_SIZE), BF16),),
        )
        grad_attn_all, summed = grad_attn_all.reshape(all_rows, D), summed.reshape(MICRO, count, D)
    else:
        grad_attn_all = gather_tokens(grad_attn).reshape(all_rows, D)
        summed = sum_tokens(nn(inner, down_w))
        grad_mixed = nt(grad_attn_all, out_w).astype(BF16)
    block_out = (hidden + summed).astype(BF16)
    gu_rows = scatter_columns(gu_term, rows)
    down_rows = scatter_rows(down_term, rows)
    grad_mixed = grad_mixed.reshape(seq, MICRO, count, -1)
    grad_q, grad_kv = attend_back(kept, grad_mixed, starts, cosine, sine, heads)
    if sharing > 1:
        groups = [[g * sharing + k for k in range(sharing)] for g in range(seq // sharing)]
        grad_kv = lax.psum(grad_kv, "seq", axis_index_groups=groups)
        grad_kv = jnp.where(lax.axis_index("seq") % sharing == 0, grad_kv, 0.0)
    grad_k, grad_v = grad_kv[..., :HEAD_SIZE], grad_kv[..., HEAD_SIZE:]
    half = HEAD_SIZE // 2
    swapped = jnp.concatenate([grad_k[..., half:], grad_k[..., :half]], axis=-1)
    table = (seq, 1, count, HEAD_SIZE)
    grad_k = grad_k * cosine.reshape(table) - swapped * sine.reshape(table)
    grad_qkv = jnp.concatenate([grad_q, grad_k.astype(BF16), grad_v.astype(BF16)], axis=-1)
    grad_qkv = grad_qkv.reshape(all_rows, -1)
    if lined:
        (grad_norm_one,) = exchange(4, seq, terms=(chunked(grad_qkv), qkv_w), transposed=True)
        grad_norm_one = grad_norm_one.reshape(MICRO, count, D)
    else:
        grad_norm_one = sum_tokens(nt(grad_qkv, qkv_w))
    gain_one = jnp.sum(grad_norm_one * x * inv_one, axis=(0, 1))
    input_grad = (grad_hidden + norm_back(grad_norm_one, x, inv_one, gain_all[0])).astype(BF16)
    gain_terms = jnp.stack([gain_one, gain_two]).reshape(2, devices, -1).transpose(1, 0, 2)
    gain_grad = jnp.sum(
        lax.all_to_all(gain_terms, BOTH, split_axis=0, concat_axis=0, tiled=True), axis=0
    )
    qkv_rows = scatter_columns(tn(normed, grad_qkv), rows)
    out_rows = scatter_rows(tn(mixed, grad_attn_all), rows)

    def column_blocks(part):
        return part.transpose(2, 0, 1, 3).reshape(rows, -1, PRECOND_ORDER)

    def row_blocks(part):
        return part.transpose(1, 0, 2).reshape(rows, -1, PRECOND_ORDER)

    def shared_blocks(part):
        return column_blocks(part[:, ::sharing])

    q_width = heads * HEAD_SIZE
    attn_grad = jnp.concatenate(
        [
            column_blocks(qkv_rows[..., :q_width]),
            shared_blocks(qkv_rows[..., q_width : q_width + HEAD_SIZE]),
            shared_blocks(qkv_rows[..., q_width + HEAD_SIZE :]),
            row_blocks(out_rows),
        ],
        axis=1,
    )
    ffn_grad = jnp.concatenate(
        [
            column_blocks(gu_rows[..., :feed]),
            column_blocks(gu_rows[..., feed:]),
            row_blocks(down_rows),
        ],
        axis=1,
    )

    grad_all = jnp.concatenate([attn_grad, ffn_grad], axis=1)
    slots = left_stats.shape[0]
    blocks = grad_all.shape[1]
    slot_table = jnp.arange(slots)[:, None] + jnp.arange(devices)[None, :] * slots
    slot_match = owner_slot[None, None, :] == slot_table[:, :, None]
    slot_block = jnp.sum(jnp.where(slot_match, jnp.arange(blocks)[None, None, :], 0), axis=-1)
    filled = jnp.any(slot_match, axis=-1)
    by_block = jnp.transpose(grad_all, (1, 0, 2))
    outgoing = jnp.where(filled[:, :, None, None], by_block[slot_block], 0.0).astype(BF16)
    held = lax.all_to_all(outgoing, BOTH, split_axis=1, concat_axis=1, tiled=True)
    held = held.reshape(slots, PRECOND_ORDER, PRECOND_ORDER)
    own_slots = lax.axis_index(BOTH) * slots + jnp.arange(slots)
    owned = jnp.any(owner_slot[None, :] == own_slots[:, None], axis=-1)[:, None, None]

    def batched(a, b, a_dim, b_dim):
        return lax.dot_general(
            a, b, (((a_dim,), (b_dim,)), ((0,), (0,))), preferred_element_type=F32
        )

    step = batched(left_root.astype(BF16), held, 2, 1)
    step = batched(step.astype(BF16), right_root.astype(BF16), 2, 1).astype(BF16)
    returned = lax.all_to_all(
        step.reshape(slots, devices, rows, PRECOND_ORDER),
        BOTH,
        split_axis=1,
        concat_axis=1,
        tiled=True,
    )
    normalizer = 1.0 * MICRO * fsdp * length * PRECOND_ORDER
    gram_left = batched(held, held, 2, 2) / normalizer
    gram_right = batched(held, held, 1, 1) / normalizer
    new_left = jnp.where(
        owned, STAT_DECAY * left_stats + (1.0 - STAT_DECAY) * gram_left, left_stats
    )
    new_right = jnp.where(
        owned, STAT_DECAY * right_stats + (1.0 - STAT_DECAY) * gram_right, right_stats
    )
    flat = jnp.transpose(returned, (1, 0, 2, 3)).reshape(devices * slots, rows, PRECOND_ORDER)
    update = jnp.transpose(flat[owner_slot], (1, 0, 2)).astype(F32)
    attn_count = attn_blocks.shape[1]
    return (
        block_out[:, None],
        input_grad[:, None],
        attn_grad.astype(F32),
        ffn_grad.astype(F32),
        gain_grad,
        attn_blocks - STEP_RATE * update[:, :attn_count],
        ffn_blocks - STEP_RATE * update[:, attn_count:],
        gains - GAIN_RATE * gain_grad,
        new_left,
        new_right,
    )


def solution(mesh):
    by_token = P(None, "fsdp", "seq", None)
    by_row = P(BOTH, None, None)
    by_gain = P(None, BOTH)
    return jax.shard_map(
        shards,
        mesh=mesh,
        in_specs=(
            by_token,
            by_token,
            P(None, "fsdp", None),
            by_row,
            by_row,
            by_gain,
            by_row,
            by_row,
            by_row,
            by_row,
            P(),
        ),
        out_specs=(
            by_token,
            by_token,
            by_row,
            by_row,
            by_gain,
            by_row,
            by_row,
            by_gain,
            by_row,
            by_row,
        ),
        check_vma=False,
    )
```

```python
import functools

import jax
import jax.numpy as jnp
from jax import lax
from jax.experimental import pallas as pl
from jax.experimental.pallas import tpu as pltpu
from jax.sharding import PartitionSpec as P

D = 2048
QUERY_HEADS = 16
KEY_VALUE_HEADS = 8
HEAD_SIZE = 128
FF = 8192
PRECOND_ORDER = 1024
MICRO = 2
PIECE = 256

EPSILON = 1e-06
ROTARY_BASE = 1000000.0
STAT_DECAY = 0.5
STEP_RATE = 1.0
GAIN_RATE = 0.001

F32 = jnp.float32
BF16 = jnp.bfloat16
BOTH = ("fsdp", "seq")
SCALE = HEAD_SIZE ** (-0.5)
QUERY_ROWS = 256
D_BLK = D // PRECOND_ORDER
FF_BLK = FF // PRECOND_ORDER
VMEM_LIMIT = 56 * 1024 * 1024
TILE = 512
LINE_CHIPS = 4
MESH = pl.DeviceIdType.MESH


def dot(a, b, contract):
    return lax.dot_general(a, b, (contract, ((), ())), preferred_element_type=F32)


def nn(a, b):
    return dot(a, b, ((1,), (0,)))


def nt(a, b):
    return dot(a, b, ((1,), (1,)))


def tn(a, b):
    return dot(a, b, ((0,), (0,)))


def swap_seq(array, axis):
    return lax.all_to_all(array, "seq", split_axis=axis, concat_axis=axis, tiled=True)


def sum_fsdp(array):
    arrived = lax.all_to_all(array, "fsdp", split_axis=0, concat_axis=0, tiled=True)
    return jnp.sum(arrived.astype(F32), axis=0).astype(BF16)


def column_parts(shard, parts):
    rows = shard.shape[0]
    columns = shard.shape[1] // D_BLK * PRECOND_ORDER // parts
    return shard.reshape(rows, D_BLK, parts, columns).transpose(2, 1, 0, 3)


def gather_columns(parts):
    swapped = swap_seq(parts, 0)
    whole = lax.all_gather(swapped, "fsdp", axis=0, tiled=False)
    return whole.transpose(2, 0, 1, 3, 4).reshape(D, parts.shape[-1])


def sum_columns(term, rows):
    seq, fsdp = lax.axis_size("seq"), lax.axis_size("fsdp")
    shaped = term.reshape(D_BLK, fsdp, seq, rows, term.shape[1]).transpose(1, 0, 2, 3, 4)
    return sum_fsdp(shaped)


def swap_columns(summed):
    return swap_seq(summed, 1)


def gather_rows(shard):
    seq, fsdp = lax.axis_size("seq"), lax.axis_size("fsdp")
    rows, groups = shard.shape[:2]
    by_group = shard.reshape(rows, groups, D).transpose(1, 0, 2)
    if groups == seq:
        swapped = swap_seq(by_group, 0)
        whole = lax.all_gather(swapped, "fsdp", axis=0, tiled=False)
        return whole.reshape(PRECOND_ORDER, D)
    whole = lax.all_gather(by_group, "fsdp", axis=1, tiled=False)
    pieces = whole.reshape(seq, groups * fsdp // seq, rows, D)
    swapped = swap_seq(pieces, 0)
    return swapped.transpose(1, 0, 2, 3).reshape(groups * PRECOND_ORDER // seq, D)


def rows_whole(groups):
    return groups == lax.axis_size("seq")


def sum_rows(term, rows):
    seq, fsdp = lax.axis_size("seq"), lax.axis_size("fsdp")
    groups = term.shape[0] * seq // PRECOND_ORDER
    if rows_whole(groups):
        return sum_fsdp(term.reshape(fsdp, seq, rows, D))
    pieces = term.reshape(groups * fsdp // seq, seq, rows, D).transpose(1, 0, 2, 3)
    return swap_seq(pieces, 0)


def swap_rows(part, rows):
    seq, fsdp = lax.axis_size("seq"), lax.axis_size("fsdp")
    if len(part.shape) == 3:
        return swap_seq(part, 0)
    return sum_fsdp(part.reshape(-1, fsdp, rows, D).transpose(1, 0, 2, 3))


def turn(value, cosine, sine, sign):
    return value * cosine + sign * (pltpu.roll(value, HEAD_SIZE // 2, 1) * sine)


def piece_index(starts_ref, micro, position, outside):
    index = jnp.full(position.shape, outside, jnp.int32)
    for piece in range(starts_ref.shape[1]):
        start = starts_ref[micro, piece]
        index = jnp.where((position >= start) & (position < start + PIECE), piece, index)
    return index


def softmax_rows(queries, keys, starts_ref, micro, first):
    rows, length = queries.shape[0], keys.shape[0]
    query_pos = first + lax.broadcasted_iota(jnp.int32, (rows, 1), 0)
    key_pos = lax.broadcasted_iota(jnp.int32, (1, length), 1)
    same = piece_index(starts_ref, micro, query_pos, -1) == piece_index(
        starts_ref, micro, key_pos, -2
    )
    scores = jnp.where((key_pos <= query_pos) | same, nt(queries, keys) * SCALE, -1e30)
    exponent = jnp.exp(scores - jnp.max(scores, axis=1, keepdims=True))
    return exponent / jnp.sum(exponent, axis=1, keepdims=True)


def query_blocks(length):
    rows = min(QUERY_ROWS, length)
    for first in range(0, length, rows):
        yield first, rows, min(length, first + rows + PIECE)


def attend_kernel(heads, starts_ref, qkv_ref, cosine_ref, sine_ref, kept_ref, mixed_ref, k_ref, v_ref):
    micro = pl.program_id(0)
    parts, _, rows, _ = qkv_ref.shape
    length = parts * rows
    cosine, sine = cosine_ref[...], sine_ref[...]

    def columns(head):
        return pl.ds(head * HEAD_SIZE, HEAD_SIZE)

    def turned(head):
        value = qkv_ref[:, 0, :, columns(head)].reshape(length, HEAD_SIZE)
        return turn(value, cosine, sine, 1.0).astype(BF16)

    def keep(head, value):
        kept_ref[:, 0, :, columns(head)] = value.reshape(parts, rows, HEAD_SIZE)

    k_ref[...] = turned(heads)
    v_ref[...] = qkv_ref[:, 0, :, columns(heads + 1)].reshape(length, HEAD_SIZE).astype(BF16)
    keep(heads, k_ref[...])
    keep(heads + 1, v_ref[...])
    for head in range(heads):
        queries = turned(head)
        keep(head, queries)
        for first, count, seen in query_blocks(length):
            chances = softmax_rows(
                queries[first : first + count], k_ref[:seen], starts_ref, micro, first
            )
            mixed = nn(chances.astype(BF16), v_ref[:seen]).astype(BF16)
            mixed_ref[first // rows : (first + count) // rows, 0, :, columns(head)] = mixed.reshape(
                count // rows, rows, HEAD_SIZE
            )


def attend_back_kernel(
    heads, starts_ref, kept_ref, grad_ref, cosine_ref, sine_ref, q_out, kv_out, k_acc, v_acc
):
    micro = pl.program_id(0)
    parts, _, rows, _ = kept_ref.shape
    length = parts * rows

    def columns(head):
        return pl.ds(head * HEAD_SIZE, HEAD_SIZE)

    keys = kept_ref[:, 0, :, columns(heads)].reshape(length, HEAD_SIZE)
    values = kept_ref[:, 0, :, columns(heads + 1)].reshape(length, HEAD_SIZE)
    k_acc[...] = jnp.zeros_like(k_acc)
    v_acc[...] = jnp.zeros_like(v_acc)
    for head in range(heads):
        for first, count, seen in query_blocks(length):
            span = slice(first // rows, (first + count) // rows)
            queries = kept_ref[span, 0, :, columns(head)].reshape(count, HEAD_SIZE)
            grads = grad_ref[span, 0, :, columns(head)].reshape(count, HEAD_SIZE)
            chances = softmax_rows(queries, keys[:seen], starts_ref, micro, first)
            grad_prob = nt(grads, values[:seen])
            inner = jnp.sum(grad_prob * chances, axis=1, keepdims=True)
            grad_scores = (chances * (grad_prob - inner)).astype(BF16)
            grad_queries = nn(grad_scores, keys[:seen]) * SCALE
            place = slice(first, first + count)
            q_out[span, 0, :, columns(head)] = (
                turn(grad_queries, cosine_ref[place], sine_ref[place], -1.0)
                .astype(BF16)
                .reshape(count // rows, rows, HEAD_SIZE)
            )
            k_acc[:seen] += tn(grad_scores, queries)
            v_acc[:seen] += tn(chances.astype(BF16), grads)
    kv_out[:, 0, :, columns(0)] = (k_acc[...] * SCALE).reshape(parts, rows, HEAD_SIZE)
    kv_out[:, 0, :, columns(1)] = v_acc[...].reshape(parts, rows, HEAD_SIZE)


def per_micro(parts, rows, columns):
    return pl.BlockSpec((parts, 1, rows, columns), lambda micro: (0, micro, 0, 0))


def whole_table(length):
    return pl.BlockSpec((length, HEAD_SIZE), lambda micro: (0, 0))


def attend(qkv, starts, cosine, sine, heads):
    parts, _, rows, width = qkv.shape
    length = parts * rows
    return pl.pallas_call(
        functools.partial(attend_kernel, heads),
        grid=(MICRO,),
        out_shape=(
            jax.ShapeDtypeStruct(qkv.shape, BF16),
            jax.ShapeDtypeStruct((parts, MICRO, rows, heads * HEAD_SIZE), BF16),
        ),
        in_specs=[
            pl.BlockSpec(memory_space=pltpu.SMEM),
            per_micro(parts, rows, width),
            whole_table(length),
            whole_table(length),
        ],
        out_specs=(per_micro(parts, rows, width), per_micro(parts, rows, heads * HEAD_SIZE)),
        scratch_shapes=[
            pltpu.VMEM((length, HEAD_SIZE), BF16),
            pltpu.VMEM((length, HEAD_SIZE), BF16),
        ],
        compiler_params=pltpu.CompilerParams(vmem_limit_bytes=VMEM_LIMIT),
        cost_estimate=pl.CostEstimate(
            flops=MICRO * heads * 4 * length * length * HEAD_SIZE,
            bytes_accessed=8 * qkv.size,
            transcendentals=MICRO * heads * length * length,
        ),
        name="attend",
    )(starts, qkv, cosine, sine)


def attend_back(kept, grad_mixed, starts, cosine, sine, heads):
    parts, _, rows, width = kept.shape
    length = parts * rows
    return pl.pallas_call(
        functools.partial(attend_back_kernel, heads),
        grid=(MICRO,),
        out_shape=(
            jax.ShapeDtypeStruct(grad_mixed.shape, BF16),
            jax.ShapeDtypeStruct((parts, MICRO, rows, 2 * HEAD_SIZE), F32),
        ),
        in_specs=[
            pl.BlockSpec(memory_space=pltpu.SMEM),
            per_micro(parts, rows, width),
            per_micro(parts, rows, heads * HEAD_SIZE),
            whole_table(length),
            whole_table(length),
        ],
        out_specs=(
            per_micro(parts, rows, heads * HEAD_SIZE),
            per_micro(parts, rows, 2 * HEAD_SIZE),
        ),
        scratch_shapes=[
            pltpu.VMEM((length, HEAD_SIZE), F32),
            pltpu.VMEM((length, HEAD_SIZE), F32),
        ],
        compiler_params=pltpu.CompilerParams(vmem_limit_bytes=VMEM_LIMIT),
        cost_estimate=pl.CostEstimate(
            flops=MICRO * heads * 10 * length * length * HEAD_SIZE,
            bytes_accessed=8 * kept.size,
            transcendentals=MICRO * heads * length * length,
        ),
        name="attend_back",
    )(starts, kept, grad_mixed, cosine, sine)


def rotary_tables(length):
    half = HEAD_SIZE // 2
    frequency = jnp.power(ROTARY_BASE, -(jnp.arange(half).astype(F32) * (2.0 / HEAD_SIZE)))
    angles = jnp.arange(length).astype(F32)[:, None] * frequency[None, :]
    cosine, sine = jnp.cos(angles), jnp.sin(angles)
    return jnp.concatenate([cosine, cosine], axis=1), jnp.concatenate([-sine, sine], axis=1)


class Place:
    def __init__(self, seq, fsdp):
        self.seq, self.fsdp = seq, fsdp
        self.count = seq // 2
        self.me = lax.axis_index("seq")
        self.row = lax.axis_index("fsdp")
        self.spot = lax.div(self.me, 2)
        self.core = lax.rem(self.me, 2)
        self.sibling = self.me + 1 - 2 * self.core
        first = jnp.where(2 * self.spot < self.count, 1, -1)
        self.ways = [Way(self, number, sign) for number, sign in enumerate((first, -first))]

    def greet(self, everyone):
        barrier = pltpu.get_barrier_semaphore()

        def signal(device, axis="seq"):
            pl.semaphore_signal(barrier, inc=1, device_id={axis: device}, device_id_type=MESH)

        if everyone:
            for number in range(1, self.seq):
                signal(lax.rem(self.me + number, self.seq))
            for number in range(1, self.fsdp):
                signal(lax.rem(self.row + number, self.fsdp), "fsdp")
            pl.semaphore_wait(barrier, self.seq + self.fsdp - 2)
            return
        signal(self.sibling)
        for sign, there in ((-1, self.spot > 0), (1, self.spot < self.count - 1)):

            @pl.when(there)
            def _():
                signal(self.me + 2 * sign)

        ends = (self.spot > 0).astype(jnp.int32) + (self.spot < self.count - 1).astype(jnp.int32)
        pl.semaphore_wait(barrier, 1 + ends)


class Way:
    def __init__(self, place, number, sign):
        self.number = number
        self.lane = lax.div(1 - sign, 2)
        self.last = place.count - 1
        self.sign = sign
        self.behind = jnp.where(sign == 1, place.spot, self.last - place.spot)
        self.ahead = place.me + 2 * sign

    def spot(self, mirrored):
        return jnp.where(self.sign == 1, mirrored, self.last - mirrored)


class Gather:
    def __init__(self, place, own, chunks, sems):
        self.place, self.own, self.chunks = place, own, chunks
        self.send, self.recv, self.give, self.take, self.own_sem = sems
        self.steps = place.count - 1

    def index(self, way, upstream):
        return 2 * way.spot(way.behind - upstream) + self.place.core

    def copy(self, way, step, index, source):
        return pltpu.make_async_remote_copy(
            src_ref=source,
            dst_ref=self.chunks.at[index],
            send_sem=self.send.at[way.lane, step],
            recv_sem=self.recv.at[way.lane, step],
            device_id={"seq": way.ahead},
            device_id_type=MESH,
        )

    def line(self, way, step):
        index = self.index(way, step)
        return self.copy(way, step, index, self.own if step == 0 else self.chunks.at[index])

    def arrival(self, way, step):
        index = self.index(way, step + 1)
        return self.copy(way, step, index, self.chunks.at[index])

    def pair(self, index, event):
        return pltpu.make_async_remote_copy(
            src_ref=self.own if event == 0 else self.chunks.at[index],
            dst_ref=self.chunks.at[index],
            send_sem=self.give.at[event],
            recv_sem=self.take.at[event],
            device_id={"seq": self.place.sibling},
            device_id_type=MESH,
        )

    def other(self, index):
        return index + 1 - 2 * self.place.core

    def event(self, way, step):
        return 1 + way.number * self.steps + step

    def sends(self, way, step):
        return (way.behind < self.steps) & (way.behind >= step)

    def arrives(self, way, step):
        return way.behind > step

    def start(self):
        me = self.place.me
        mine = pltpu.make_async_copy(self.own, self.chunks.at[me], self.own_sem)
        mine.start()
        for way in self.place.ways:

            @pl.when(self.sends(way, 0))
            def _():
                self.line(way, 0).start()

        self.pair(me, 0).start()
        mine.wait()

    def visit_own(self, visit):
        me = self.place.me
        visit(me)
        self.pair(self.other(me), 0).wait_recv()
        visit(self.other(me))

    def receive(self, way, step):
        @pl.when(self.arrives(way, step))
        def _():
            index = self.index(way, step + 1)
            self.arrival(way, step).wait_recv()
            self.pair(index, self.event(way, step)).start()

    def visit_step(self, way, step, visit):
        @pl.when(self.arrives(way, step))
        def _():
            index = self.index(way, step + 1)
            visit(index)
            self.pair(self.other(index), self.event(way, step)).wait_recv()
            visit(self.other(index))

    def finish(self):
        self.pair(self.place.me, 0).wait_send()
        for way in self.place.ways:
            for step in range(self.steps):

                @pl.when(self.arrives(way, step))
                def _():
                    self.pair(self.index(way, step + 1), self.event(way, step)).wait_send()


class Scatter:
    def __init__(self, place, term, buffers, sems):
        self.place, self.term = place, term
        self.stage, self.lent, self.slots, self.work = buffers
        self.send, self.recv, self.give, self.take = sems
        self.steps = place.count - 1
        self.tiles = D // TILE

    def for_tiles(self, body):
        @pl.loop(0, self.tiles)
        def _(number):
            body(pl.ds(pl.multiple_of(number * TILE, TILE), TILE))

    def lend_copy(self, spot):
        return pltpu.make_async_remote_copy(
            src_ref=self.stage.at[spot],
            dst_ref=self.lent.at[spot],
            send_sem=self.give.at[spot],
            recv_sem=self.take.at[spot],
            device_id={"seq": self.place.sibling},
            device_id_type=MESH,
        )

    def lend(self, spot):
        index = 2 * spot + 1 - self.place.core

        def body(columns):
            self.stage[spot, :, columns] = self.term(index, columns).astype(BF16)

        self.for_tiles(body)
        self.lend_copy(spot).start()

    def own_term(self, spot):
        index = 2 * spot + self.place.core
        self.lend_copy(spot).wait_recv()

        def body(columns):
            self.work[:, columns] = self.term(index, columns) + self.lent[spot, :, columns].astype(F32)

        self.for_tiles(body)

    def line(self, way, step):
        return pltpu.make_async_remote_copy(
            src_ref=self.slots.at[way.lane, step],
            dst_ref=self.slots.at[way.lane, step],
            send_sem=self.send.at[way.lane, step],
            recv_sem=self.recv.at[way.lane, step],
            device_id={"seq": way.ahead},
            device_id_type=MESH,
        )

    def sends(self, way, step):
        return (step >= 0) & (step < self.steps - way.behind)

    def lend_step(self, way, step):
        @pl.when(self.sends(way, step))
        def _():
            self.lend(way.spot(self.steps - step))

    def prepare(self, way, step):
        @pl.when(self.sends(way, step))
        def _():
            self.own_term(way.spot(self.steps - step))

            @pl.when(way.behind > 0)
            def _():
                self.line(way, step).wait_recv()

                def body(columns):
                    slot = self.slots[way.lane, step, :, columns].astype(F32)
                    self.slots[way.lane, step, :, columns] = (self.work[:, columns] + slot).astype(BF16)

                self.for_tiles(body)

            @pl.when(way.behind == 0)
            def _():
                def body(columns):
                    self.slots[way.lane, step, :, columns] = self.work[:, columns].astype(BF16)

                self.for_tiles(body)

    def own_sum(self, total):
        self.own_term(self.place.spot)
        total[...] = self.work[...]
        for way in self.place.ways:

            @pl.when(way.behind > 0)
            def _():
                step = self.steps - way.behind
                self.line(way, step).wait_recv()

                def body(columns):
                    total[:, columns] += self.slots[way.lane, step, :, columns].astype(F32)

                self.for_tiles(body)

    def finish(self):
        for spot in range(self.place.count):
            self.lend_copy(spot).wait_send()


class Spread:
    def __init__(self, place, parts, whole, sems):
        self.place, self.parts, self.whole = place, parts, whole
        self.send, self.recv, self.on_send, self.on_recv, self.own_sem = sems
        self.seq, self.fsdp = place.seq, place.fsdp
        self.rows = parts.shape[-2]

    def region(self, fsdp, seq):
        row = pl.multiple_of((fsdp * self.seq + seq) * self.rows, self.rows)
        where = pl.ds(row, self.rows)
        return self.whole.at[where, :] if len(self.whole.shape) == 2 else self.whole.at[:, where, :]

    def shift(self, index, by, size):
        return lax.rem(index + by + size, size)

    def to_seq(self, number):
        place = self.place
        peer = self.shift(place.me, number, self.seq)
        return pltpu.make_async_remote_copy(
            src_ref=self.parts.at[peer],
            dst_ref=self.region(place.row, place.me),
            send_sem=self.send.at[number],
            recv_sem=self.recv.at[number],
            device_id={"seq": peer},
            device_id_type=MESH,
        )

    def from_seq(self, number):
        place = self.place
        here = self.region(place.row, self.shift(place.me, -number, self.seq))
        return pltpu.make_async_remote_copy(
            src_ref=here,
            dst_ref=here,
            send_sem=self.send.at[number],
            recv_sem=self.recv.at[number],
            device_id={"seq": self.shift(place.me, number, self.seq)},
            device_id_type=MESH,
        )

    def own(self):
        place = self.place
        return pltpu.make_async_copy(
            self.parts.at[place.me], self.region(place.row, place.me), self.own_sem
        )

    def to_fsdp(self, hop, number, sender):
        place = self.place
        here = self.region(sender, self.shift(place.me, -number, self.seq))
        return pltpu.make_async_remote_copy(
            src_ref=here,
            dst_ref=here,
            send_sem=self.on_send.at[hop, number],
            recv_sem=self.on_recv.at[hop, number],
            device_id={"fsdp": self.shift(place.row, hop, self.fsdp)},
            device_id_type=MESH,
        )

    def start(self):
        self.own().start()
        for number in range(1, self.seq):
            self.to_seq(number).start()

    def pass_on(self, number):
        if number == 0:
            self.own().wait()
        else:
            self.from_seq(number).wait_recv()
        for hop in range(1, self.fsdp):
            self.to_fsdp(hop, number, self.place.row).start()

    def arrive(self):
        for hop in range(1, self.fsdp):
            for number in range(self.seq):
                self.to_fsdp(hop, number, self.shift(self.place.row, -hop, self.fsdp)).wait_recv()

    def finish(self):
        for number in range(1, self.seq):
            self.to_seq(number).wait_send()
        for hop in range(1, self.fsdp):
            for number in range(self.seq):
                self.to_fsdp(hop, number, self.place.row).wait_send()


def exchange_kernel(plan, *refs):
    refs = list(refs)

    def take(number):
        taken, refs[:] = refs[:number], refs[number:]
        return taken

    gathers, scatters, spreads = plan["gathers"], plan["scatters"], plan["spreads"]
    own = take(gathers)
    parts = take(spreads)
    loads = take(plan["loads"])
    total = take(scatters)
    kept = take(plan["keeps"])
    wholes = take(spreads)
    more_out = take(plan["outs"])
    place = Place(plan["seq"], plan["fsdp"])
    gather = scatter = None
    if gathers:
        chunks = take(1)[0]
        gather = Gather(place, own[0], chunks, take(5))
        keep_sem = take(plan["keeps"])
    landed = take(plan["loads"])
    load_sem = take(1)[0]
    if scatters:
        a_ref, b_ref = landed[:2]

        def term(index, columns):
            if plan["transposed"]:
                return nt(a_ref[index], b_ref[columns, :])
            return nn(a_ref[index], b_ref[:, columns])

        scatter = Scatter(place, term, take(4), take(4))
    spread_list, spread_kept = [], []
    for parts_ref, whole_ref, in_vmem in zip(parts, wholes, plan["in_vmem"]):
        landing = take(1)[0] if in_vmem else whole_ref
        spread_list.append(Spread(place, parts_ref, landing, take(5)))
        if in_vmem:
            spread_kept.append(pltpu.make_async_copy(landing, whole_ref, take(1)[0]))
            landed.append(landing)
    staged = take(plan["outs"])
    out_sem = take(1)[0] if plan["outs"] else None
    more_in = landed[2 * scatters :]

    def out_copy(number, index):
        return pltpu.make_async_copy(
            staged[number].at[index], more_out[number].at[index], out_sem.at[number, index]
        )

    def keep_copy(index):
        return pltpu.make_async_copy(chunks.at[index], kept[0].at[index], keep_sem[0].at[index])

    def see(index):
        if kept:
            keep_copy(index).start()
        if plan["visit"] is not None:
            plan["visit"](index, chunks, more_in, staged)
            for number in range(plan["outs"]):
                out_copy(number, index).start()

    load_copies = [
        pltpu.make_async_copy(source, target, load_sem.at[number])
        for number, (source, target) in enumerate(zip(loads, landed))
    ]
    for copy in load_copies:
        copy.start()
    place.greet(spreads > 0)
    if gather:
        gather.start()
    for spread in spread_list:
        spread.start()
    for copy in load_copies:
        copy.wait()
    slots = place.count
    if scatter:
        for step in range(slots - 1):
            for way in place.ways:
                scatter.lend_step(way, step)
            if not gather:
                break
        if gather:
            scatter.lend(place.spot)
    passes = [[] for _ in range(slots)]
    for number in range(place.seq if spread_list else 0):
        passes[number * slots // place.seq].append(number)
    if spread_kept:
        passes[0] = [number for group in passes for number in group]
        passes[1:] = [[] for _ in range(slots - 1)]
    for number in passes[0]:
        for spread in spread_list:
            spread.pass_on(number)

    def sent(way, slot):
        if gather:

            @pl.when(gather.sends(way, slot))
            def _():
                gather.line(way, slot).wait_send()

        if scatter:
            step = slot - way.behind - gathers

            @pl.when(scatter.sends(way, step))
            def _():
                scatter.line(way, step).wait_send()

    first = gathers
    for slot in range(first, slots):
        for way in place.ways:
            if gather:
                gather.receive(way, slot - 1)
            if scatter:
                scatter.prepare(way, slot - way.behind - gathers)
            if slot > 0:
                sent(way, slot - 1)
            if gather:

                @pl.when(gather.sends(way, slot))
                def _():
                    gather.line(way, slot).start()

            if scatter:
                step = slot - way.behind - gathers

                @pl.when(scatter.sends(way, step))
                def _():
                    scatter.line(way, step).start()

        for number in passes[slot] if slot else []:
            for spread in spread_list:
                spread.pass_on(number)
        if scatter and not gather:
            if slot + 1 < slots - 1:
                for way in place.ways:
                    scatter.lend_step(way, slot + 1)
            elif slot + 1 == slots - 1:
                scatter.lend(place.spot)
        if gather:
            if slot == first:
                if spread_kept:
                    for spread in spread_list:
                        spread.arrive()
                    for copy in spread_kept:
                        copy.start()
                gather.visit_own(see)
            for way in place.ways:
                gather.visit_step(way, slot - 1, see)
    for way in place.ways:
        sent(way, slots - 1)
    if scatter:
        scatter.own_sum(total[0])
        scatter.finish()
    if gather:
        gather.finish()
    for spread in spread_list:
        if not spread_kept:
            spread.arrive()
        spread.finish()
    for copy in spread_kept:
        copy.wait()
    for index in range(place.seq):
        if kept:
            keep_copy(index).wait()
        for number in range(plan["outs"]):
            out_copy(number, index).wait()


def exchange(
    number,
    sizes,
    own=None,
    terms=None,
    transposed=False,
    keep=True,
    parts=(),
    wholes=(),
    in_vmem=(),
    visit=None,
    extra_in=(),
    extra_out=(),
):
    fsdp, seq = sizes
    gathers, scatters = int(own is not None), int(terms is not None)
    keeps = int(keep and gathers)
    chips = seq // 2
    rows = own.shape[0] if gathers else terms[0].shape[1]
    vmem, anywhere = pl.BlockSpec(memory_space=pltpu.VMEM), pl.BlockSpec(memory_space=pl.ANY)
    loads = (list(terms) if scatters else []) + list(extra_in)
    operands, in_specs, outs, out_specs, scratch = [], [], [], [], []
    dma = pltpu.SemaphoreType.DMA
    if gathers:
        operands.append(own)
        in_specs.append(vmem)
    operands += list(parts) + loads
    in_specs += [anywhere] * (len(parts) + len(loads))
    if scatters:
        outs.append(jax.ShapeDtypeStruct((rows, D), F32))
        out_specs.append(vmem)
    if keeps:
        outs.append(jax.ShapeDtypeStruct((seq, rows, D), BF16))
    outs += [jax.ShapeDtypeStruct(shape, BF16) for shape in wholes] + list(extra_out)
    out_specs += [anywhere] * (len(outs) - len(out_specs))
    if gathers:
        scratch += [
            pltpu.VMEM((seq, rows, D), BF16),
            dma((2, chips - 1)),
            dma((2, chips - 1)),
            dma((2 * chips - 1,)),
            dma((2 * chips - 1,)),
            dma,
        ] + [dma((seq,))] * keeps
    scratch += [pltpu.VMEM(load.shape, load.dtype) for load in loads] + [dma((max(1, len(loads)),))]
    if scatters:
        scratch += [
            pltpu.VMEM((chips, rows, D), BF16),
            pltpu.VMEM((chips, rows, D), BF16),
            pltpu.VMEM((2, chips - 1, rows, D), BF16),
            pltpu.VMEM((rows, D), F32),
            dma((2, chips - 1)),
            dma((2, chips - 1)),
            dma((chips,)),
            dma((chips,)),
        ]
    for shape, landing in zip(wholes, in_vmem):
        scratch += [pltpu.VMEM(shape, BF16)] * landing
        scratch += [dma((seq,)), dma((seq,)), dma((fsdp, seq)), dma((fsdp, seq)), dma]
        scratch += [dma] * landing
    scratch += [pltpu.VMEM(out.shape, out.dtype) for out in extra_out]
    if extra_out:
        scratch.append(dma((len(extra_out), seq)))
    plan = dict(
        seq=seq,
        fsdp=fsdp,
        gathers=gathers,
        scatters=scatters,
        keeps=keeps,
        spreads=len(parts),
        in_vmem=in_vmem,
        loads=len(loads),
        outs=len(extra_out),
        transposed=transposed,
        visit=visit,
    )
    return pl.pallas_call(
        functools.partial(exchange_kernel, plan),
        out_shape=tuple(outs),
        in_specs=in_specs,
        out_specs=tuple(out_specs),
        scratch_shapes=scratch,
        compiler_params=pltpu.CompilerParams(
            collective_id=number, has_side_effects=True, vmem_limit_bytes=VMEM_LIMIT
        ),
        cost_estimate=pl.CostEstimate(
            flops=0, bytes_accessed=300 * 1000 * 1000, transcendentals=0
        ),
        name="exchange_" + str(number),
    )(*operands)


def norm_visit(index, chunks, more_in, more_out):
    gain_ref, weight_ref = more_in
    normed_ref, qkv_ref = more_out
    value = chunks[index].astype(F32)
    normed = (value * inverse_rms(value) * gain_ref[0:1, :]).astype(BF16)
    normed_ref[index] = normed
    half = PRECOND_ORDER
    qkv_ref[index] = nn(normed[:, :half], weight_ref[0]) + nn(normed[:, half:], weight_ref[1])


def feed_visit(index, chunks, more_in, more_out):
    cot_ref, gu_ref, down_ref = more_in
    inner_ref, grad_ref = more_out
    feed = down_ref.shape[0]
    width = min(256, feed)

    @pl.loop(0, feed // width)
    def _(number):
        start = pl.multiple_of(number * width, width)
        gate_columns = pl.ds(start, width)
        up_columns = pl.ds(pl.multiple_of(feed + start, width), width)
        rows = chunks[index]
        gate = nn(rows, gu_ref[:, gate_columns])
        up = nn(rows, gu_ref[:, up_columns])
        grad_inner = nt(cot_ref[index], down_ref[gate_columns, :])
        sigma = jax.nn.sigmoid(gate)
        inner_ref[index, :, gate_columns] = (gate * sigma * up).astype(BF16)
        grad_ref[index, :, gate_columns] = (
            grad_inner * up * sigma * (1.0 + gate * (1.0 - sigma))
        ).astype(BF16)
        grad_ref[index, :, up_columns] = (grad_inner * gate * sigma).astype(BF16)


def weight_shape(columns):
    return (D_BLK, PRECOND_ORDER, columns)


def mixed_visit(index, chunks, more_in, more_out):
    more_out[0][index] = nt(chunks[index], more_in[0][...]).astype(BF16)


def inverse_rms(value):
    return lax.rsqrt(jnp.mean(value * value, axis=-1, keepdims=True) + EPSILON)


def norm_back(grad, value, inverse, gain):
    scaled = grad * gain
    return inverse * scaled - value * inverse**3 * jnp.mean(scaled * value, axis=-1, keepdims=True)


def shards(
    tokens,
    cotangent,
    piece_starts,
    attn_blocks,
    ffn_blocks,
    gains,
    left_stats,
    right_stats,
    left_root,
    right_root,
    owner_slot,
):
    fsdp, seq = lax.axis_size("fsdp"), lax.axis_size("seq")
    devices = fsdp * seq
    rows = attn_blocks.shape[0]
    count = tokens.shape[2]
    length = seq * count
    heads = QUERY_HEADS // seq
    sharing = max(1, seq // KEY_VALUE_HEADS)
    all_rows = MICRO * length
    feed = FF // seq
    starts = piece_starts[:, 0]
    cosine, sine = rotary_tables(length)

    def gather_tokens(value):
        return lax.all_gather(value, "seq", axis=0, tiled=False)

    def sum_tokens(term):
        term = term.astype(BF16).reshape(seq, MICRO, count, D)
        return lax.psum_scatter(term, "seq", scatter_dimension=0, tiled=False).astype(F32)

    q_cut = D_BLK * QUERY_HEADS * HEAD_SIZE // PRECOND_ORDER
    kv_blk = D_BLK * KEY_VALUE_HEADS * HEAD_SIZE // PRECOND_ORDER
    k_cut, v_cut = q_cut + kv_blk, q_cut + 2 * kv_blk
    attn_low, ffn_low = attn_blocks.astype(BF16), ffn_blocks.astype(BF16)

    def shared_parts(shard):
        return jnp.repeat(column_parts(shard, seq // sharing), sharing, axis=0)

    chunk_rows = MICRO * count
    sizes = (fsdp, seq)
    lined = seq == 2 * LINE_CHIPS

    def chunked(value):
        return value.reshape(seq, chunk_rows, -1)

    def like_chunks(columns, dtype=BF16):
        return jax.ShapeDtypeStruct((seq, chunk_rows, columns), dtype)

    gain_all = lax.all_to_all(
        jnp.broadcast_to(gains.astype(BF16)[None], (devices,) + gains.shape),
        BOTH,
        split_axis=0,
        concat_axis=0,
        tiled=True,
    )
    gain_all = gain_all.transpose(1, 0, 2).reshape(2, D).astype(F32)
    qkv_parts = jnp.concatenate(
        [
            column_parts(attn_low[:, :q_cut], seq),
            shared_parts(attn_low[:, q_cut:k_cut]),
            shared_parts(attn_low[:, k_cut:v_cut]),
        ],
        axis=-1,
    )
    gu_cut = D_BLK * FF_BLK
    gu_parts = jnp.concatenate(
        [
            column_parts(ffn_low[:, :gu_cut], seq),
            column_parts(ffn_low[:, gu_cut : 2 * gu_cut], seq),
        ],
        axis=-1,
    )
    down_shard = ffn_low[:, 2 * gu_cut :].reshape(rows, FF_BLK, D_BLK, PRECOND_ORDER)
    out_w = gather_rows(attn_low[:, v_cut:].reshape(rows, -1, D_BLK, PRECOND_ORDER))

    x = tokens[:, 0].astype(F32)
    inv_one = inverse_rms(x)
    cot_own = cotangent[:, 0].reshape(chunk_rows, D)
    if lined:
        qkv_w, normed, qkv = exchange(
            0,
            sizes,
            own=tokens[:, 0].reshape(chunk_rows, D),
            keep=False,
            parts=(qkv_parts,),
            wholes=(weight_shape(qkv_parts.shape[-1]),),
            in_vmem=(1,),
            visit=norm_visit,
            extra_in=(gain_all,),
            extra_out=(like_chunks(D), like_chunks(qkv_parts.shape[-1], F32)),
        )
        qkv_w, normed = qkv_w.reshape(D, -1), normed.reshape(all_rows, D)
    else:
        qkv_w = gather_columns(qkv_parts)
        x_all = gather_tokens(tokens[:, 0]).astype(F32)
        normed = (x_all * inverse_rms(x_all) * gain_all[0]).astype(BF16).reshape(all_rows, D)
        qkv = nn(normed, qkv_w)
    kept, mixed = attend(qkv.reshape(seq, MICRO, count, -1), starts, cosine, sine, heads)
    mixed = mixed.reshape(all_rows, heads * HEAD_SIZE)
    if lined:
        summed, cot_all, gu_w, down_w = exchange(
            1,
            sizes,
            own=cot_own,
            terms=(chunked(mixed), out_w),
            parts=(gu_parts, down_shard.reshape(rows, FF_BLK, D).transpose(1, 0, 2)),
            wholes=(weight_shape(2 * feed), (PRECOND_ORDER, D)),
            in_vmem=(0, 0),
        )
        gu_w = gu_w.reshape(D, 2 * feed)
        cot_all, summed = cot_all.reshape(all_rows, D), summed.reshape(MICRO, count, D)
    else:
        gu_w, down_w = gather_columns(gu_parts), gather_rows(down_shard)
        cot_all = gather_tokens(cotangent[:, 0]).reshape(all_rows, D)
        summed = sum_tokens(nn(mixed, out_w))
    hidden = x + summed
    inv_two = inverse_rms(hidden)
    normed_two = (hidden * inv_two * gain_all[1]).astype(BF16)
    if lined:
        normed_two_all, inner, grad_gu = exchange(
            2,
            sizes,
            own=normed_two.reshape(chunk_rows, D),
            visit=feed_visit,
            extra_in=(chunked(cot_all), gu_w, down_w),
            extra_out=(like_chunks(feed), like_chunks(2 * feed)),
        )
        normed_two_all = normed_two_all.reshape(all_rows, D)
        inner, grad_gu = inner.reshape(all_rows, feed), grad_gu.reshape(all_rows, 2 * feed)
    else:
        normed_two_all = gather_tokens(normed_two).reshape(all_rows, D)
        gate_up = nn(normed_two_all, gu_w)
        gate, up = gate_up[:, :feed], gate_up[:, feed:]
        sigma = jax.nn.sigmoid(gate)
        inner = (gate * sigma * up).astype(BF16)
        grad_inner = nt(cot_all, down_w)
        grad_gu = jnp.concatenate(
            [
                (grad_inner * up * sigma * (1.0 + gate * (1.0 - sigma))).astype(BF16),
                (grad_inner * gate * sigma).astype(BF16),
            ],
            axis=1,
        )

    gu_term = tn(normed_two_all, grad_gu).astype(BF16)
    down_term = tn(inner, cot_all).astype(BF16)
    grad_gu, gu_term, down_term = lax.optimization_barrier((grad_gu, gu_term, down_term))
    gu_sum, down_sum = sum_columns(gu_term, rows), sum_rows(down_term, rows)
    if lined:
        (grad_norm_two,) = exchange(3, sizes, terms=(chunked(grad_gu), gu_w), transposed=True)
        grad_norm_two = grad_norm_two.reshape(MICRO, count, D)
    else:
        grad_norm_two = sum_tokens(nt(grad_gu, gu_w))
    gain_two = jnp.sum(grad_norm_two * hidden * inv_two, axis=(0, 1))
    grad_hidden = cotangent[:, 0].astype(F32) + norm_back(
        grad_norm_two, hidden, inv_two, gain_all[1]
    )
    grad_attn = grad_hidden.astype(BF16)
    grad_attn, gu_sum = lax.optimization_barrier((grad_attn, gu_sum))
    if lined:
        summed, grad_attn_all, grad_mixed = exchange(
            4,
            sizes,
            own=grad_attn.reshape(chunk_rows, D),
            terms=(chunked(inner), down_w),
            visit=mixed_visit,
            extra_in=(out_w,),
            extra_out=(like_chunks(heads * HEAD_SIZE),),
        )
        grad_attn_all, summed = grad_attn_all.reshape(all_rows, D), summed.reshape(MICRO, count, D)
    else:
        grad_attn_all = gather_tokens(grad_attn).reshape(all_rows, D)
        summed = sum_tokens(nn(inner, down_w))
        grad_mixed = nt(grad_attn_all, out_w).astype(BF16)
    block_out = (hidden + summed).astype(BF16)
    out_term = tn(mixed, grad_attn_all).astype(BF16)
    grad_mixed, down_sum, out_term = lax.optimization_barrier((grad_mixed, down_sum, out_term))
    gu_rows, down_rows = swap_columns(gu_sum), swap_rows(down_sum, rows)
    out_rows = swap_rows(sum_rows(out_term, rows), rows)
    grad_mixed = grad_mixed.reshape(seq, MICRO, count, -1)
    grad_q, grad_kv = attend_back(kept, grad_mixed, starts, cosine, sine, heads)
    if sharing > 1:
        groups = [[g * sharing + k for k in range(sharing)] for g in range(seq // sharing)]
        grad_kv = lax.psum(grad_kv, "seq", axis_index_groups=groups)
        grad_kv = jnp.where(lax.axis_index("seq") % sharing == 0, grad_kv, 0.0)
    grad_k, grad_v = grad_kv[..., :HEAD_SIZE], grad_kv[..., HEAD_SIZE:]
    half = HEAD_SIZE // 2
    swapped = jnp.concatenate([grad_k[..., half:], grad_k[..., :half]], axis=-1)
    table = (seq, 1, count, HEAD_SIZE)
    grad_k = grad_k * cosine.reshape(table) - swapped * sine.reshape(table)
    grad_qkv = jnp.concatenate([grad_q, grad_k.astype(BF16), grad_v.astype(BF16)], axis=-1)
    grad_qkv = grad_qkv.reshape(all_rows, -1)
    if lined:
        (grad_norm_one,) = exchange(5, sizes, terms=(chunked(grad_qkv), qkv_w), transposed=True)
        grad_norm_one = grad_norm_one.reshape(MICRO, count, D)
    else:
        grad_norm_one = sum_tokens(nt(grad_qkv, qkv_w))
    gain_one = jnp.sum(grad_norm_one * x * inv_one, axis=(0, 1))
    input_grad = (grad_hidden + norm_back(grad_norm_one, x, inv_one, gain_all[0])).astype(BF16)
    gain_terms = jnp.stack([gain_one, gain_two]).reshape(2, devices, -1).transpose(1, 0, 2)
    gain_grad = jnp.sum(
        lax.all_to_all(gain_terms, BOTH, split_axis=0, concat_axis=0, tiled=True), axis=0
    )
    qkv_rows = swap_columns(sum_columns(tn(normed, grad_qkv).astype(BF16), rows))

    def column_blocks(part):
        return part.transpose(2, 0, 1, 3).reshape(rows, -1, PRECOND_ORDER)

    def row_blocks(part):
        return part.transpose(1, 0, 2).reshape(rows, -1, PRECOND_ORDER)

    def shared_blocks(part):
        return column_blocks(part[:, ::sharing])

    q_width = heads * HEAD_SIZE
    attn_grad = jnp.concatenate(
        [
            column_blocks(qkv_rows[..., :q_width]),
            shared_blocks(qkv_rows[..., q_width : q_width + HEAD_SIZE]),
            shared_blocks(qkv_rows[..., q_width + HEAD_SIZE :]),
            row_blocks(out_rows),
        ],
        axis=1,
    )
    ffn_grad = jnp.concatenate(
        [
            column_blocks(gu_rows[..., :feed]),
            column_blocks(gu_rows[..., feed:]),
            row_blocks(down_rows),
        ],
        axis=1,
    )

    grad_all = jnp.concatenate([attn_grad, ffn_grad], axis=1)
    slots = left_stats.shape[0]
    blocks = grad_all.shape[1]
    slot_table = jnp.arange(slots)[:, None] + jnp.arange(devices)[None, :] * slots
    slot_match = owner_slot[None, None, :] == slot_table[:, :, None]
    slot_block = jnp.sum(jnp.where(slot_match, jnp.arange(blocks)[None, None, :], 0), axis=-1)
    filled = jnp.any(slot_match, axis=-1)
    by_block = jnp.transpose(grad_all, (1, 0, 2))
    outgoing = jnp.where(filled[:, :, None, None], by_block[slot_block], 0.0).astype(BF16)
    held = lax.all_to_all(outgoing, BOTH, split_axis=1, concat_axis=1, tiled=True)
    held = held.reshape(slots, PRECOND_ORDER, PRECOND_ORDER)
    own_slots = lax.axis_index(BOTH) * slots + jnp.arange(slots)
    owned = jnp.any(owner_slot[None, :] == own_slots[:, None], axis=-1)[:, None, None]

    def batched(a, b, a_dim, b_dim):
        return lax.dot_general(
            a, b, (((a_dim,), (b_dim,)), ((0,), (0,))), preferred_element_type=F32
        )

    step = batched(left_root.astype(BF16), held, 2, 1)
    step = batched(step.astype(BF16), right_root.astype(BF16), 2, 1).astype(BF16)
    returned = lax.all_to_all(
        step.reshape(slots, devices, rows, PRECOND_ORDER),
        BOTH,
        split_axis=1,
        concat_axis=1,
        tiled=True,
    )
    normalizer = 1.0 * MICRO * fsdp * length * PRECOND_ORDER
    gram_left = batched(held, held, 2, 2) / normalizer
    gram_right = batched(held, held, 1, 1) / normalizer
    new_left = jnp.where(
        owned, STAT_DECAY * left_stats + (1.0 - STAT_DECAY) * gram_left, left_stats
    )
    new_right = jnp.where(
        owned, STAT_DECAY * right_stats + (1.0 - STAT_DECAY) * gram_right, right_stats
    )
    flat = jnp.transpose(returned, (1, 0, 2, 3)).reshape(devices * slots, rows, PRECOND_ORDER)
    update = jnp.transpose(flat[owner_slot], (1, 0, 2)).astype(F32)
    attn_count = attn_blocks.shape[1]
    return (
        block_out[:, None],
        input_grad[:, None],
        attn_grad.astype(F32),
        ffn_grad.astype(F32),
        gain_grad,
        attn_blocks - STEP_RATE * update[:, :attn_count],
        ffn_blocks - STEP_RATE * update[:, attn_count:],
        gains - GAIN_RATE * gain_grad,
        new_left,
        new_right,
    )


def solution(mesh):
    by_token = P(None, "fsdp", "seq", None)
    by_row = P(BOTH, None, None)
    by_gain = P(None, BOTH)
    return jax.shard_map(
        shards,
        mesh=mesh,
        in_specs=(
            by_token,
            by_token,
            P(None, "fsdp", None),
            by_row,
            by_row,
            by_gain,
            by_row,
            by_row,
            by_row,
            by_row,
            P(),
        ),
        out_specs=(
            by_token,
            by_token,
            by_row,
            by_row,
            by_gain,
            by_row,
            by_row,
            by_gain,
            by_row,
            by_row,
        ),
        check_vma=False,
    )
```

```python
import functools

import jax
import jax.numpy as jnp
from jax import lax
from jax.experimental import pallas as pl
from jax.experimental.pallas import tpu as pltpu
from jax.sharding import PartitionSpec as P

D = 2048
QUERY_HEADS = 16
KEY_VALUE_HEADS = 8
HEAD_SIZE = 128
FF = 8192
PRECOND_ORDER = 1024
MICRO = 2
PIECE = 256

EPSILON = 1e-06
ROTARY_BASE = 1000000.0
STAT_DECAY = 0.5
STEP_RATE = 1.0
GAIN_RATE = 0.001

F32 = jnp.float32
BF16 = jnp.bfloat16
BOTH = ("fsdp", "seq")
SCALE = HEAD_SIZE ** (-0.5)
QUERY_ROWS = 256
D_BLK = D // PRECOND_ORDER
FF_BLK = FF // PRECOND_ORDER
VMEM_LIMIT = 56 * 1024 * 1024
TILE = 512
LINE_CHIPS = 4
MESH = pl.DeviceIdType.MESH


def dot(a, b, contract):
    return lax.dot_general(a, b, (contract, ((), ())), preferred_element_type=F32)


def nn(a, b):
    return dot(a, b, ((1,), (0,)))


def nt(a, b):
    return dot(a, b, ((1,), (1,)))


def tn(a, b):
    return dot(a, b, ((0,), (0,)))


def swap_seq(array, axis):
    return lax.all_to_all(array, "seq", split_axis=axis, concat_axis=axis, tiled=True)


def sum_parts(arrived):
    return jnp.sum(arrived.astype(F32), axis=0).astype(BF16)


def sum_fsdp(array):
    return sum_parts(lax.all_to_all(array, "fsdp", split_axis=0, concat_axis=0, tiled=True))


def column_parts(shard, parts):
    rows = shard.shape[0]
    columns = shard.shape[1] // D_BLK * PRECOND_ORDER // parts
    return shard.reshape(rows, D_BLK, parts, columns).transpose(2, 1, 0, 3)


def gather_columns(parts):
    swapped = swap_seq(parts, 0)
    whole = lax.all_gather(swapped, "fsdp", axis=0, tiled=False)
    return whole.transpose(2, 0, 1, 3, 4).reshape(D, parts.shape[-1])


def sum_columns(term, rows):
    seq, fsdp = lax.axis_size("seq"), lax.axis_size("fsdp")
    shaped = term.reshape(D_BLK, fsdp, seq, rows, term.shape[1]).transpose(1, 0, 2, 3, 4)
    return sum_fsdp(shaped)


def swap_columns(summed):
    return swap_seq(summed, 1)


def gather_rows(shard):
    seq, fsdp = lax.axis_size("seq"), lax.axis_size("fsdp")
    rows, groups = shard.shape[:2]
    by_group = shard.reshape(rows, groups, D).transpose(1, 0, 2)
    if groups == seq:
        swapped = swap_seq(by_group, 0)
        whole = lax.all_gather(swapped, "fsdp", axis=0, tiled=False)
        return whole.reshape(PRECOND_ORDER, D)
    whole = lax.all_gather(by_group, "fsdp", axis=1, tiled=False)
    pieces = whole.reshape(seq, groups * fsdp // seq, rows, D)
    swapped = swap_seq(pieces, 0)
    return swapped.transpose(1, 0, 2, 3).reshape(groups * PRECOND_ORDER // seq, D)


def rows_whole(groups):
    return groups == lax.axis_size("seq")


def sum_rows(term, rows):
    seq, fsdp = lax.axis_size("seq"), lax.axis_size("fsdp")
    groups = term.shape[0] * seq // PRECOND_ORDER
    if rows_whole(groups):
        return sum_fsdp(term.reshape(fsdp, seq, rows, D))
    pieces = term.reshape(groups * fsdp // seq, seq, rows, D).transpose(1, 0, 2, 3)
    return swap_seq(pieces, 0)


def swap_rows(part, rows):
    seq, fsdp = lax.axis_size("seq"), lax.axis_size("fsdp")
    if len(part.shape) == 3:
        return swap_seq(part, 0)
    return sum_fsdp(part.reshape(-1, fsdp, rows, D).transpose(1, 0, 2, 3))


def turn(value, cosine, sine, sign):
    return value * cosine + sign * (pltpu.roll(value, HEAD_SIZE // 2, 1) * sine)


def piece_index(starts_ref, micro, position, outside):
    index = jnp.full(position.shape, outside, jnp.int32)
    for piece in range(starts_ref.shape[1]):
        start = starts_ref[micro, piece]
        index = jnp.where((position >= start) & (position < start + PIECE), piece, index)
    return index


def softmax_rows(queries, keys, starts_ref, micro, first):
    rows, length = queries.shape[0], keys.shape[0]
    query_pos = first + lax.broadcasted_iota(jnp.int32, (rows, 1), 0)
    key_pos = lax.broadcasted_iota(jnp.int32, (1, length), 1)
    same = piece_index(starts_ref, micro, query_pos, -1) == piece_index(
        starts_ref, micro, key_pos, -2
    )
    scores = jnp.where((key_pos <= query_pos) | same, nt(queries, keys) * SCALE, -1e30)
    exponent = jnp.exp(scores - jnp.max(scores, axis=1, keepdims=True))
    return exponent / jnp.sum(exponent, axis=1, keepdims=True)


def query_blocks(length):
    rows = min(QUERY_ROWS, length)
    for first in range(0, length, rows):
        yield first, rows, min(length, first + rows + PIECE)


def attend_kernel(heads, starts_ref, qkv_ref, cosine_ref, sine_ref, kept_ref, mixed_ref, k_ref, v_ref):
    micro = pl.program_id(0)
    parts, _, rows, _ = qkv_ref.shape
    length = parts * rows
    cosine, sine = cosine_ref[...], sine_ref[...]

    def columns(head):
        return pl.ds(head * HEAD_SIZE, HEAD_SIZE)

    def turned(head):
        value = qkv_ref[:, 0, :, columns(head)].reshape(length, HEAD_SIZE)
        return turn(value, cosine, sine, 1.0).astype(BF16)

    def keep(head, value):
        kept_ref[:, 0, :, columns(head)] = value.reshape(parts, rows, HEAD_SIZE)

    k_ref[...] = turned(heads)
    v_ref[...] = qkv_ref[:, 0, :, columns(heads + 1)].reshape(length, HEAD_SIZE).astype(BF16)
    keep(heads, k_ref[...])
    keep(heads + 1, v_ref[...])
    for head in range(heads):
        queries = turned(head)
        keep(head, queries)
        for first, count, seen in query_blocks(length):
            chances = softmax_rows(
                queries[first : first + count], k_ref[:seen], starts_ref, micro, first
            )
            mixed = nn(chances.astype(BF16), v_ref[:seen]).astype(BF16)
            mixed_ref[first // rows : (first + count) // rows, 0, :, columns(head)] = mixed.reshape(
                count // rows, rows, HEAD_SIZE
            )


def attend_back_kernel(
    heads, starts_ref, kept_ref, grad_ref, cosine_ref, sine_ref, q_out, kv_out, k_acc, v_acc
):
    micro = pl.program_id(0)
    parts, _, rows, _ = kept_ref.shape
    length = parts * rows

    def columns(head):
        return pl.ds(head * HEAD_SIZE, HEAD_SIZE)

    keys = kept_ref[:, 0, :, columns(heads)].reshape(length, HEAD_SIZE)
    values = kept_ref[:, 0, :, columns(heads + 1)].reshape(length, HEAD_SIZE)
    k_acc[...] = jnp.zeros_like(k_acc)
    v_acc[...] = jnp.zeros_like(v_acc)
    for head in range(heads):
        for first, count, seen in query_blocks(length):
            span = slice(first // rows, (first + count) // rows)
            queries = kept_ref[span, 0, :, columns(head)].reshape(count, HEAD_SIZE)
            grads = grad_ref[span, 0, :, columns(head)].reshape(count, HEAD_SIZE)
            chances = softmax_rows(queries, keys[:seen], starts_ref, micro, first)
            grad_prob = nt(grads, values[:seen])
            inner = jnp.sum(grad_prob * chances, axis=1, keepdims=True)
            grad_scores = (chances * (grad_prob - inner)).astype(BF16)
            grad_queries = nn(grad_scores, keys[:seen]) * SCALE
            place = slice(first, first + count)
            q_out[span, 0, :, columns(head)] = (
                turn(grad_queries, cosine_ref[place], sine_ref[place], -1.0)
                .astype(BF16)
                .reshape(count // rows, rows, HEAD_SIZE)
            )
            k_acc[:seen] += tn(grad_scores, queries)
            v_acc[:seen] += tn(chances.astype(BF16), grads)
    kv_out[:, 0, :, columns(0)] = (k_acc[...] * SCALE).reshape(parts, rows, HEAD_SIZE)
    kv_out[:, 0, :, columns(1)] = v_acc[...].reshape(parts, rows, HEAD_SIZE)


def per_micro(parts, rows, columns):
    return pl.BlockSpec((parts, 1, rows, columns), lambda micro: (0, micro, 0, 0))


def whole_table(length):
    return pl.BlockSpec((length, HEAD_SIZE), lambda micro: (0, 0))


def attend(qkv, starts, cosine, sine, heads):
    parts, _, rows, width = qkv.shape
    length = parts * rows
    return pl.pallas_call(
        functools.partial(attend_kernel, heads),
        grid=(MICRO,),
        out_shape=(
            jax.ShapeDtypeStruct(qkv.shape, BF16),
            jax.ShapeDtypeStruct((parts, MICRO, rows, heads * HEAD_SIZE), BF16),
        ),
        in_specs=[
            pl.BlockSpec(memory_space=pltpu.SMEM),
            per_micro(parts, rows, width),
            whole_table(length),
            whole_table(length),
        ],
        out_specs=(per_micro(parts, rows, width), per_micro(parts, rows, heads * HEAD_SIZE)),
        scratch_shapes=[
            pltpu.VMEM((length, HEAD_SIZE), BF16),
            pltpu.VMEM((length, HEAD_SIZE), BF16),
        ],
        compiler_params=pltpu.CompilerParams(vmem_limit_bytes=VMEM_LIMIT),
        cost_estimate=pl.CostEstimate(
            flops=MICRO * heads * 4 * length * length * HEAD_SIZE,
            bytes_accessed=8 * qkv.size,
            transcendentals=MICRO * heads * length * length,
        ),
        name="attend",
    )(starts, qkv, cosine, sine)


def attend_back(kept, grad_mixed, starts, cosine, sine, heads):
    parts, _, rows, width = kept.shape
    length = parts * rows
    return pl.pallas_call(
        functools.partial(attend_back_kernel, heads),
        grid=(MICRO,),
        out_shape=(
            jax.ShapeDtypeStruct(grad_mixed.shape, BF16),
            jax.ShapeDtypeStruct((parts, MICRO, rows, 2 * HEAD_SIZE), F32),
        ),
        in_specs=[
            pl.BlockSpec(memory_space=pltpu.SMEM),
            per_micro(parts, rows, width),
            per_micro(parts, rows, heads * HEAD_SIZE),
            whole_table(length),
            whole_table(length),
        ],
        out_specs=(
            per_micro(parts, rows, heads * HEAD_SIZE),
            per_micro(parts, rows, 2 * HEAD_SIZE),
        ),
        scratch_shapes=[
            pltpu.VMEM((length, HEAD_SIZE), F32),
            pltpu.VMEM((length, HEAD_SIZE), F32),
        ],
        compiler_params=pltpu.CompilerParams(vmem_limit_bytes=VMEM_LIMIT),
        cost_estimate=pl.CostEstimate(
            flops=MICRO * heads * 10 * length * length * HEAD_SIZE,
            bytes_accessed=8 * kept.size,
            transcendentals=MICRO * heads * length * length,
        ),
        name="attend_back",
    )(starts, kept, grad_mixed, cosine, sine)


def rotary_tables(length):
    half = HEAD_SIZE // 2
    frequency = jnp.power(ROTARY_BASE, -(jnp.arange(half).astype(F32) * (2.0 / HEAD_SIZE)))
    angles = jnp.arange(length).astype(F32)[:, None] * frequency[None, :]
    cosine, sine = jnp.cos(angles), jnp.sin(angles)
    return jnp.concatenate([cosine, cosine], axis=1), jnp.concatenate([-sine, sine], axis=1)


class Place:
    def __init__(self, seq, fsdp):
        self.seq, self.fsdp = seq, fsdp
        self.count = seq // 2
        self.me = lax.axis_index("seq")
        self.row = lax.axis_index("fsdp")
        self.spot = lax.div(self.me, 2)
        self.core = lax.rem(self.me, 2)
        self.sibling = self.me + 1 - 2 * self.core
        first = jnp.where(2 * self.spot < self.count, 1, -1)
        self.ways = [Way(self, number, sign) for number, sign in enumerate((first, -first))]

    def greet(self, everyone):
        barrier = pltpu.get_barrier_semaphore()

        def signal(device, axis="seq"):
            pl.semaphore_signal(barrier, inc=1, device_id={axis: device}, device_id_type=MESH)

        if everyone:
            for number in range(1, self.seq):
                signal(lax.rem(self.me + number, self.seq))
            for number in range(1, self.fsdp):
                signal(lax.rem(self.row + number, self.fsdp), "fsdp")
            pl.semaphore_wait(barrier, self.seq + self.fsdp - 2)
            return
        signal(self.sibling)
        for sign, there in ((-1, self.spot > 0), (1, self.spot < self.count - 1)):

            @pl.when(there)
            def _():
                signal(self.me + 2 * sign)

        ends = (self.spot > 0).astype(jnp.int32) + (self.spot < self.count - 1).astype(jnp.int32)
        pl.semaphore_wait(barrier, 1 + ends)


class Way:
    def __init__(self, place, number, sign):
        self.number = number
        self.lane = lax.div(1 - sign, 2)
        self.last = place.count - 1
        self.sign = sign
        self.behind = jnp.where(sign == 1, place.spot, self.last - place.spot)
        self.ahead = place.me + 2 * sign

    def spot(self, mirrored):
        return jnp.where(self.sign == 1, mirrored, self.last - mirrored)


class Gather:
    def __init__(self, place, own, chunks, sems):
        self.place, self.own, self.chunks = place, own, chunks
        self.send, self.recv, self.give, self.take, self.own_sem = sems
        self.steps = place.count - 1

    def index(self, way, upstream):
        return 2 * way.spot(way.behind - upstream) + self.place.core

    def copy(self, way, step, index, source):
        return pltpu.make_async_remote_copy(
            src_ref=source,
            dst_ref=self.chunks.at[index],
            send_sem=self.send.at[way.lane, step],
            recv_sem=self.recv.at[way.lane, step],
            device_id={"seq": way.ahead},
            device_id_type=MESH,
        )

    def line(self, way, step):
        index = self.index(way, step)
        return self.copy(way, step, index, self.own if step == 0 else self.chunks.at[index])

    def arrival(self, way, step):
        index = self.index(way, step + 1)
        return self.copy(way, step, index, self.chunks.at[index])

    def pair(self, index, event):
        return pltpu.make_async_remote_copy(
            src_ref=self.own if event == 0 else self.chunks.at[index],
            dst_ref=self.chunks.at[index],
            send_sem=self.give.at[event],
            recv_sem=self.take.at[event],
            device_id={"seq": self.place.sibling},
            device_id_type=MESH,
        )

    def other(self, index):
        return index + 1 - 2 * self.place.core

    def event(self, way, step):
        return 1 + way.number * self.steps + step

    def sends(self, way, step):
        return (way.behind < self.steps) & (way.behind >= step)

    def arrives(self, way, step):
        return way.behind > step

    def start(self):
        me = self.place.me
        mine = pltpu.make_async_copy(self.own, self.chunks.at[me], self.own_sem)
        mine.start()
        for way in self.place.ways:

            @pl.when(self.sends(way, 0))
            def _():
                self.line(way, 0).start()

        self.pair(me, 0).start()
        mine.wait()

    def visit_own(self, visit):
        me = self.place.me
        visit(me)
        self.pair(self.other(me), 0).wait_recv()
        visit(self.other(me))

    def receive(self, way, step):
        @pl.when(self.arrives(way, step))
        def _():
            index = self.index(way, step + 1)
            self.arrival(way, step).wait_recv()
            self.pair(index, self.event(way, step)).start()

    def visit_step(self, way, step, visit):
        @pl.when(self.arrives(way, step))
        def _():
            index = self.index(way, step + 1)
            visit(index)
            self.pair(self.other(index), self.event(way, step)).wait_recv()
            visit(self.other(index))

    def finish(self):
        self.pair(self.place.me, 0).wait_send()
        for way in self.place.ways:
            for step in range(self.steps):

                @pl.when(self.arrives(way, step))
                def _():
                    self.pair(self.index(way, step + 1), self.event(way, step)).wait_send()


class Scatter:
    def __init__(self, place, term, buffers, sems):
        self.place, self.term = place, term
        self.stage, self.lent, self.slots, self.work = buffers
        self.send, self.recv, self.give, self.take = sems
        self.steps = place.count - 1
        self.tiles = D // TILE

    def for_tiles(self, body):
        @pl.loop(0, self.tiles)
        def _(number):
            body(pl.ds(pl.multiple_of(number * TILE, TILE), TILE))

    def lend_copy(self, spot):
        return pltpu.make_async_remote_copy(
            src_ref=self.stage.at[spot],
            dst_ref=self.lent.at[spot],
            send_sem=self.give.at[spot],
            recv_sem=self.take.at[spot],
            device_id={"seq": self.place.sibling},
            device_id_type=MESH,
        )

    def lend(self, spot):
        index = 2 * spot + 1 - self.place.core

        def body(columns):
            self.stage[spot, :, columns] = self.term(index, columns).astype(BF16)

        self.for_tiles(body)
        self.lend_copy(spot).start()

    def own_term(self, spot):
        index = 2 * spot + self.place.core
        self.lend_copy(spot).wait_recv()

        def body(columns):
            self.work[:, columns] = self.term(index, columns) + self.lent[spot, :, columns].astype(F32)

        self.for_tiles(body)

    def line(self, way, step):
        return pltpu.make_async_remote_copy(
            src_ref=self.slots.at[way.lane, step],
            dst_ref=self.slots.at[way.lane, step],
            send_sem=self.send.at[way.lane, step],
            recv_sem=self.recv.at[way.lane, step],
            device_id={"seq": way.ahead},
            device_id_type=MESH,
        )

    def sends(self, way, step):
        return (step >= 0) & (step < self.steps - way.behind)

    def lend_step(self, way, step):
        @pl.when(self.sends(way, step))
        def _():
            self.lend(way.spot(self.steps - step))

    def prepare(self, way, step):
        @pl.when(self.sends(way, step))
        def _():
            self.own_term(way.spot(self.steps - step))

            @pl.when(way.behind > 0)
            def _():
                self.line(way, step).wait_recv()

                def body(columns):
                    slot = self.slots[way.lane, step, :, columns].astype(F32)
                    self.slots[way.lane, step, :, columns] = (self.work[:, columns] + slot).astype(BF16)

                self.for_tiles(body)

            @pl.when(way.behind == 0)
            def _():
                def body(columns):
                    self.slots[way.lane, step, :, columns] = self.work[:, columns].astype(BF16)

                self.for_tiles(body)

    def own_sum(self, total):
        self.own_term(self.place.spot)
        total[...] = self.work[...]
        for way in self.place.ways:

            @pl.when(way.behind > 0)
            def _():
                step = self.steps - way.behind
                self.line(way, step).wait_recv()

                def body(columns):
                    total[:, columns] += self.slots[way.lane, step, :, columns].astype(F32)

                self.for_tiles(body)

    def finish(self):
        for spot in range(self.place.count):
            self.lend_copy(spot).wait_send()


class Spread:
    def __init__(self, place, parts, whole, sems):
        self.place, self.parts, self.whole = place, parts, whole
        self.send, self.recv, self.on_send, self.on_recv, self.own_sem = sems
        self.seq, self.fsdp = place.seq, place.fsdp
        self.rows = parts.shape[-2]

    def region(self, fsdp, seq):
        row = pl.multiple_of((fsdp * self.seq + seq) * self.rows, self.rows)
        where = pl.ds(row, self.rows)
        return self.whole.at[where, :] if len(self.whole.shape) == 2 else self.whole.at[:, where, :]

    def shift(self, index, by, size):
        return lax.rem(index + by + size, size)

    def to_seq(self, number):
        place = self.place
        peer = self.shift(place.me, number, self.seq)
        return pltpu.make_async_remote_copy(
            src_ref=self.parts.at[peer],
            dst_ref=self.region(place.row, place.me),
            send_sem=self.send.at[number],
            recv_sem=self.recv.at[number],
            device_id={"seq": peer},
            device_id_type=MESH,
        )

    def from_seq(self, number):
        place = self.place
        here = self.region(place.row, self.shift(place.me, -number, self.seq))
        return pltpu.make_async_remote_copy(
            src_ref=here,
            dst_ref=here,
            send_sem=self.send.at[number],
            recv_sem=self.recv.at[number],
            device_id={"seq": self.shift(place.me, number, self.seq)},
            device_id_type=MESH,
        )

    def own(self):
        place = self.place
        return pltpu.make_async_copy(
            self.parts.at[place.me], self.region(place.row, place.me), self.own_sem
        )

    def to_fsdp(self, hop, number, sender):
        place = self.place
        here = self.region(sender, self.shift(place.me, -number, self.seq))
        return pltpu.make_async_remote_copy(
            src_ref=here,
            dst_ref=here,
            send_sem=self.on_send.at[hop, number],
            recv_sem=self.on_recv.at[hop, number],
            device_id={"fsdp": self.shift(place.row, hop, self.fsdp)},
            device_id_type=MESH,
        )

    def start(self):
        self.own().start()
        for number in range(1, self.seq):
            self.to_seq(number).start()

    def pass_on(self, number):
        if number == 0:
            self.own().wait()
        else:
            self.from_seq(number).wait_recv()
        for hop in range(1, self.fsdp):
            self.to_fsdp(hop, number, self.place.row).start()

    def arrive(self):
        for hop in range(1, self.fsdp):
            for number in range(self.seq):
                self.to_fsdp(hop, number, self.shift(self.place.row, -hop, self.fsdp)).wait_recv()

    def finish(self):
        for number in range(1, self.seq):
            self.to_seq(number).wait_send()
        for hop in range(1, self.fsdp):
            for number in range(self.seq):
                self.to_fsdp(hop, number, self.place.row).wait_send()


class Direct:
    def __init__(self, place, axis, source, target, sems):
        self.axis, self.source, self.target = axis, source, target
        self.size, self.me = (
            (place.seq, place.me) if axis == "seq" else (place.fsdp, place.row)
        )
        self.send, self.recv, self.own_sem = sems

    def shift(self, hop):
        return lax.rem(self.me + hop + self.size, self.size)

    def own(self):
        return pltpu.make_async_copy(self.source(self.me), self.target(self.me), self.own_sem)

    def copy(self, hop, source, target):
        return pltpu.make_async_remote_copy(
            src_ref=source,
            dst_ref=target,
            send_sem=self.send.at[hop],
            recv_sem=self.recv.at[hop],
            device_id={self.axis: self.shift(hop)},
            device_id_type=MESH,
        )

    def outgoing(self, hop):
        return self.copy(hop, self.source(self.shift(hop)), self.target(self.me))

    def arrival(self, hop):
        here = self.target(self.shift(-hop))
        return self.copy(hop, here, here)

    def start(self):
        self.own().start()
        for hop in range(1, self.size):
            self.outgoing(hop).start()

    def finish(self):
        self.own().wait()
        for hop in range(1, self.size):
            self.arrival(hop).wait_recv()
            self.outgoing(hop).wait_send()


def row_region(whole, index, rows):
    where = pl.ds(pl.multiple_of(index * rows, rows), rows)
    return whole.at[where, :] if len(whole.shape) == 2 else whole.at[:, where, :]


def make_direct(place, axis, form, part, whole, sems):
    if form == "swap":
        return Direct(place, axis, lambda peer: part.at[peer], lambda peer: whole.at[peer], sems)
    rows = part.shape[-2]
    if form == "rows":
        return Direct(
            place, axis, lambda peer: part.at[peer], lambda peer: row_region(whole, peer, rows), sems
        )
    return Direct(place, axis, lambda peer: part, lambda peer: row_region(whole, peer, rows), sems)


class OutSpread:
    def __init__(self, place, parts, whole, sems):
        self.place, self.parts, self.whole = place, parts, whole
        self.send, self.recv, self.on_send, self.on_recv, self.own_sem = sems
        self.holds = lax.rem(place.me, place.fsdp) == place.row

    def rows(self, index):
        return row_region(self.whole, index, self.parts.shape[1])

    def peer(self, group):
        return group * self.place.fsdp + self.place.row

    def to_seq(self, group):
        return pltpu.make_async_remote_copy(
            src_ref=self.parts.at[group],
            dst_ref=self.rows(self.place.me),
            send_sem=self.send.at[group],
            recv_sem=self.recv.at[self.place.me],
            device_id={"seq": self.peer(group)},
            device_id_type=MESH,
        )

    def own(self, group):
        return pltpu.make_async_copy(
            self.parts.at[group], self.rows(self.place.me), self.own_sem
        )

    def from_seq(self, sender):
        return pltpu.make_async_remote_copy(
            src_ref=self.rows(sender),
            dst_ref=self.rows(sender),
            send_sem=self.send.at[0],
            recv_sem=self.recv.at[sender],
            device_id={"seq": self.place.sibling},
            device_id_type=MESH,
        )

    def to_fsdp(self, hop):
        return pltpu.make_async_remote_copy(
            src_ref=self.whole,
            dst_ref=self.whole,
            send_sem=self.on_send.at[hop],
            recv_sem=self.on_recv,
            device_id={"fsdp": lax.rem(self.place.row + hop, self.place.fsdp)},
            device_id_type=MESH,
        )

    def start(self):
        for group in range(self.parts.shape[0]):

            @pl.when(self.peer(group) == self.place.me)
            def _():
                self.own(group).start()

            @pl.when(self.peer(group) != self.place.me)
            def _():
                self.to_seq(group).start()

    def pass_on(self):
        @pl.when(self.holds)
        def _():
            for sender in range(self.place.seq):

                @pl.when(self.place.me != sender)
                def _():
                    self.from_seq(sender).wait_recv()

            self.own(0).wait()
            for hop in range(1, self.place.fsdp):
                self.to_fsdp(hop).start()

    def finish(self):
        for group in range(self.parts.shape[0]):

            @pl.when(self.peer(group) != self.place.me)
            def _():
                self.to_seq(group).wait_send()

        @pl.when(self.holds)
        def _():
            for hop in range(1, self.place.fsdp):
                self.to_fsdp(hop).wait_send()

        @pl.when(jnp.logical_not(self.holds))
        def _():
            self.to_fsdp(1).wait_recv()


class FeedTerms:
    def __init__(self, sources, values, targets, buffers, sems):
        (self.normed, self.inner), (self.cot, self.grad) = sources, values
        self.down_out, self.gu_out = targets
        self.tile_in, self.tile_out = buffers
        self.in_sem, self.out_sem = sems
        self.width = self.tile_in.shape[-1]
        self.parts = self.down_out.shape[0]
        self.down_tiles = self.inner.shape[-1] // self.width
        self.tiles = self.down_tiles + D // self.width
        self.stored = []

    def load(self, tile):
        slot = tile % 2
        down = tile < self.down_tiles
        source = self.inner if down else self.normed
        start = (tile if down else tile - self.down_tiles) * self.width
        return pltpu.make_async_copy(
            source.at[:, :, pl.ds(start, self.width)], self.tile_in.at[slot], self.in_sem.at[slot]
        )

    def store(self, tile):
        slot = tile % 2
        if tile < self.down_tiles:
            target = self.down_out.at[tile]
        else:
            index = tile - self.down_tiles
            target = self.gu_out.at[index % self.parts, index // self.parts]
        return pltpu.make_async_copy(self.tile_out.at[slot], target, self.out_sem.at[slot])

    def run(self, tile):
        slot = tile % 2
        if tile == 0:
            self.load(0).start()
        self.load(tile).wait()
        if tile + 1 < self.tiles:
            self.load(tile + 1).start()
        if tile >= 2:
            self.store(tile - 2).wait()
        value = self.cot if tile < self.down_tiles else self.grad

        @pl.loop(0, value.shape[-1] // TILE)
        def _(number):
            columns = pl.ds(pl.multiple_of(number * TILE, TILE), TILE)
            left = self.tile_in[slot].reshape(-1, self.width)
            right = value[:, :, columns].reshape(-1, TILE)
            self.tile_out[slot, :, columns] = tn(left, right).astype(BF16)

        self.store(tile).start()


def exchange_kernel(plan, *refs):
    refs = list(refs)

    def take(number):
        taken, refs[:] = refs[:number], refs[number:]
        return taken

    gathers, scatters, spreads = plan["gathers"], plan["scatters"], plan["spreads"]
    directs, outers, feeds = plan["directs"], plan["outers"], plan["feeds"]
    own = take(gathers)
    parts = take(spreads)
    direct_parts = take(len(directs))
    out_parts = take(outers)
    feed_in = take(2 * feeds)
    loads = take(plan["loads"])
    total = take(scatters)
    kept = take(plan["keeps"])
    wholes = take(spreads)
    direct_wholes = take(len(directs))
    out_wholes = take(outers)
    feed_out = take(3 * feeds)
    more_out = take(plan["outs"])
    place = Place(plan["seq"], plan["fsdp"])
    gather = scatter = None
    if gathers:
        chunks = take(1)[0]
        gather = Gather(place, own[0], chunks, take(5))
        keep_sem = take(plan["keeps"])
    landed = take(plan["loads"])
    load_sem = take(1)[0]
    if scatters:
        a_ref, b_ref = landed[:2]

        def term(index, columns):
            if plan["transposed"]:
                return nt(a_ref[index], b_ref[columns, :])
            return nn(a_ref[index], b_ref[:, columns])

        scatter = Scatter(place, term, take(4), take(4))
    spread_list, spread_kept = [], []
    for parts_ref, whole_ref, in_vmem in zip(parts, wholes, plan["in_vmem"]):
        landing = take(1)[0] if in_vmem else whole_ref
        spread_list.append(Spread(place, parts_ref, landing, take(5)))
        if in_vmem:
            spread_kept.append(pltpu.make_async_copy(landing, whole_ref, take(1)[0]))
            landed.append(landing)
    staged = take(plan["outs"])
    out_sem = take(1)[0] if plan["outs"] else None
    more_in = landed[2 * scatters :]
    direct_list = [
        make_direct(place, axis, form, part, whole, take(3))
        for (axis, form), part, whole in zip(directs, direct_parts, direct_wholes)
    ]
    out_list = [OutSpread(place, out_parts[0], out_wholes[0], take(5))] if outers else []
    feed = None
    if feeds:
        feed = FeedTerms(feed_in, (more_in[0], a_ref), feed_out[:2], take(2), take(2))
        feed_direct = make_direct(place, "fsdp", "swap", feed_out[0], feed_out[2], take(3))

    def out_copy(number, index):
        return pltpu.make_async_copy(
            staged[number].at[index], more_out[number].at[index], out_sem.at[number, index]
        )

    def keep_copy(index):
        return pltpu.make_async_copy(chunks.at[index], kept[0].at[index], keep_sem[0].at[index])

    def see(index):
        if kept:
            keep_copy(index).start()
        if plan["visit"] is not None:
            plan["visit"](index, chunks, more_in, staged)
            for number in range(plan["outs"]):
                out_copy(number, index).start()

    load_copies = [
        pltpu.make_async_copy(source, target, load_sem.at[number])
        for number, (source, target) in enumerate(zip(loads, landed))
    ]
    for copy in load_copies:
        copy.start()
    place.greet(spreads + outers + feeds + len(directs) > 0)
    if gather:
        gather.start()
    for item in spread_list + out_list + direct_list:
        item.start()
    for copy in load_copies:
        copy.wait()
    slots = place.count
    if scatter:
        for step in range(slots - 1):
            for way in place.ways:
                scatter.lend_step(way, step)
            if not gather:
                break
        if gather:
            scatter.lend(place.spot)
    passes = [[] for _ in range(slots)]
    for number in range(place.seq):
        for spread, in_vmem in zip(spread_list, plan["in_vmem"]):
            slot = 0 if in_vmem else min(slots - 1, 1 + number * (slots - 1) // place.seq)
            passes[slot].append((spread, number))
    for spread, number in passes[0]:
        spread.pass_on(number)
    if gather and not spread_kept:
        gather.visit_own(see)
    tiles = [[] for _ in range(slots)]
    if feed:
        for tile in range(feed.tiles):
            late = 1 + (tile - feed.down_tiles) * (slots - 1) // (feed.tiles - feed.down_tiles)
            tiles[0 if tile < feed.down_tiles else min(late, slots - 1)].append(tile)

    def sent(way, slot):
        if gather:

            @pl.when(gather.sends(way, slot))
            def _():
                gather.line(way, slot).wait_send()

        if scatter:
            step = slot - way.behind - gathers

            @pl.when(scatter.sends(way, step))
            def _():
                scatter.line(way, step).wait_send()

    first = gathers
    for slot in range(first, slots):
        for way in place.ways:
            if gather:
                gather.receive(way, slot - 1)
            if scatter:
                scatter.prepare(way, slot - way.behind - gathers)
            if slot > 0:
                sent(way, slot - 1)
            if gather:

                @pl.when(gather.sends(way, slot))
                def _():
                    gather.line(way, slot).start()

            if scatter:
                step = slot - way.behind - gathers

                @pl.when(scatter.sends(way, step))
                def _():
                    scatter.line(way, step).start()

        for spread, number in passes[slot] if slot else []:
            spread.pass_on(number)
        if slot == first:
            for item in out_list:
                item.pass_on()
        for tile in tiles[slot]:
            feed.run(tile)
            if tile == feed.down_tiles + 1:
                feed_direct.start()
        if scatter and not gather:
            if slot + 1 < slots - 1:
                for way in place.ways:
                    scatter.lend_step(way, slot + 1)
            elif slot + 1 == slots - 1:
                scatter.lend(place.spot)
        if gather:
            if slot == first and spread_kept:
                for spread, in_vmem in zip(spread_list, plan["in_vmem"]):
                    if in_vmem:
                        spread.arrive()
                for copy in spread_kept:
                    copy.start()
                gather.visit_own(see)
            for way in place.ways:
                gather.visit_step(way, slot - 1, see)
    for way in place.ways:
        sent(way, slots - 1)
    if scatter:
        scatter.own_sum(total[0])
        scatter.finish()
    if gather:
        gather.finish()
    for spread, in_vmem in zip(spread_list, plan["in_vmem"]):
        if not in_vmem:
            spread.arrive()
        spread.finish()
    for item in out_list + direct_list:
        item.finish()
    if feed:
        for tile in range(max(0, feed.tiles - 2), feed.tiles):
            feed.store(tile).wait()
        feed_direct.finish()
    for copy in spread_kept:
        copy.wait()
    for index in range(place.seq):
        if kept:
            keep_copy(index).wait()
        for number in range(plan["outs"]):
            out_copy(number, index).wait()


def exchange(
    number,
    sizes,
    own=None,
    terms=None,
    transposed=False,
    keep=True,
    parts=(),
    wholes=(),
    in_vmem=(),
    directs=(),
    out_part=None,
    feed_in=(),
    visit=None,
    extra_in=(),
    extra_out=(),
):
    fsdp, seq = sizes
    gathers, scatters = int(own is not None), int(terms is not None)
    keeps = int(keep and gathers)
    chips = seq // 2
    rows = own.shape[0] if gathers else terms[0].shape[1]
    vmem, anywhere = pl.BlockSpec(memory_space=pltpu.VMEM), pl.BlockSpec(memory_space=pl.ANY)
    loads = (list(terms) if scatters else []) + list(extra_in)
    operands, in_specs, outs, out_specs, scratch = [], [], [], [], []
    dma = pltpu.SemaphoreType.DMA
    if gathers:
        operands.append(own)
        in_specs.append(vmem)
    direct_parts = [part for _, _, part, _ in directs]
    outers, feeds = int(out_part is not None), int(len(feed_in) > 0)
    passed = list(parts) + direct_parts + [out_part] * outers + list(feed_in) + loads
    operands += passed
    in_specs += [anywhere] * len(passed)
    if scatters:
        outs.append(jax.ShapeDtypeStruct((rows, D), F32))
        out_specs.append(vmem)
    if keeps:
        outs.append(jax.ShapeDtypeStruct((seq, rows, D), BF16))
    shapes = list(wholes) + [shape for _, _, _, shape in directs]
    if outers:
        shapes.append((seq * out_part.shape[1], D))
    if feeds:
        width = PRECOND_ORDER // fsdp
        feed_shape = (fsdp, width, D)
        shapes += [feed_shape, (fsdp, D // PRECOND_ORDER, width, terms[0].shape[-1]), feed_shape]
    outs += [jax.ShapeDtypeStruct(shape, BF16) for shape in shapes] + list(extra_out)
    out_specs += [anywhere] * (len(outs) - len(out_specs))
    if gathers:
        scratch += [
            pltpu.VMEM((seq, rows, D), BF16),
            dma((2, chips - 1)),
            dma((2, chips - 1)),
            dma((2 * chips - 1,)),
            dma((2 * chips - 1,)),
            dma,
        ] + [dma((seq,))] * keeps
    scratch += [pltpu.VMEM(load.shape, load.dtype) for load in loads] + [dma((max(1, len(loads)),))]
    if scatters:
        scratch += [
            pltpu.VMEM((chips, rows, D), BF16),
            pltpu.VMEM((chips, rows, D), BF16),
            pltpu.VMEM((2, chips - 1, rows, D), BF16),
            pltpu.VMEM((rows, D), F32),
            dma((2, chips - 1)),
            dma((2, chips - 1)),
            dma((chips,)),
            dma((chips,)),
        ]
    for shape, landing in zip(wholes, in_vmem):
        scratch += [pltpu.VMEM(shape, BF16)] * landing
        scratch += [dma((seq,)), dma((seq,)), dma((fsdp, seq)), dma((fsdp, seq)), dma]
        scratch += [dma] * landing
    scratch += [pltpu.VMEM(out.shape, out.dtype) for out in extra_out]
    if extra_out:
        scratch.append(dma((len(extra_out), seq)))
    for axis, _, _, _ in directs:
        size = seq if axis == "seq" else fsdp
        scratch += [dma((size,)), dma((size,)), dma]
    if outers:
        scratch += [dma((out_part.shape[0],)), dma((seq,)), dma((fsdp,)), dma, dma]
    if feeds:
        scratch += [
            pltpu.VMEM((2, seq, rows, width), BF16),
            pltpu.VMEM((2, width, D), BF16),
            dma((2,)),
            dma((2,)),
            dma((fsdp,)),
            dma((fsdp,)),
            dma,
        ]
    plan = dict(
        seq=seq,
        fsdp=fsdp,
        gathers=gathers,
        scatters=scatters,
        keeps=keeps,
        spreads=len(parts),
        in_vmem=in_vmem,
        directs=[(axis, form) for axis, form, _, _ in directs],
        outers=outers,
        feeds=feeds,
        loads=len(loads),
        outs=len(extra_out),
        transposed=transposed,
        visit=visit,
    )
    return pl.pallas_call(
        functools.partial(exchange_kernel, plan),
        out_shape=tuple(outs),
        in_specs=in_specs,
        out_specs=tuple(out_specs),
        scratch_shapes=scratch,
        compiler_params=pltpu.CompilerParams(
            collective_id=number, has_side_effects=True, vmem_limit_bytes=VMEM_LIMIT
        ),
        cost_estimate=pl.CostEstimate(
            flops=0, bytes_accessed=300 * 1000 * 1000, transcendentals=0
        ),
        name="exchange_" + str(number),
    )(*operands)


def norm_visit(index, chunks, more_in, more_out):
    gain_ref, weight_ref = more_in
    normed_ref, qkv_ref = more_out
    value = chunks[index].astype(F32)
    normed = (value * inverse_rms(value) * gain_ref[0:1, :]).astype(BF16)
    normed_ref[index] = normed
    half = PRECOND_ORDER
    qkv_ref[index] = nn(normed[:, :half], weight_ref[0]) + nn(normed[:, half:], weight_ref[1])


def feed_visit(index, chunks, more_in, more_out):
    cot_ref, gu_ref, down_ref = more_in
    inner_ref, grad_ref = more_out
    feed = down_ref.shape[0]
    width = min(256, feed)

    @pl.loop(0, feed // width)
    def _(number):
        start = pl.multiple_of(number * width, width)
        gate_columns = pl.ds(start, width)
        up_columns = pl.ds(pl.multiple_of(feed + start, width), width)
        rows = chunks[index]
        gate = nn(rows, gu_ref[:, gate_columns])
        up = nn(rows, gu_ref[:, up_columns])
        grad_inner = nt(cot_ref[index], down_ref[gate_columns, :])
        sigma = jax.nn.sigmoid(gate)
        inner_ref[index, :, gate_columns] = (gate * sigma * up).astype(BF16)
        grad_ref[index, :, gate_columns] = (
            grad_inner * up * sigma * (1.0 + gate * (1.0 - sigma))
        ).astype(BF16)
        grad_ref[index, :, up_columns] = (grad_inner * gate * sigma).astype(BF16)


def weight_shape(columns):
    return (D_BLK, PRECOND_ORDER, columns)


def mixed_visit(index, chunks, more_in, more_out):
    more_out[0][index] = nt(chunks[index], more_in[0][...]).astype(BF16)


def inverse_rms(value):
    return lax.rsqrt(jnp.mean(value * value, axis=-1, keepdims=True) + EPSILON)


def norm_back(grad, value, inverse, gain):
    scaled = grad * gain
    return inverse * scaled - value * inverse**3 * jnp.mean(scaled * value, axis=-1, keepdims=True)


def shards(
    tokens,
    cotangent,
    piece_starts,
    attn_blocks,
    ffn_blocks,
    gains,
    left_stats,
    right_stats,
    left_root,
    right_root,
    owner_slot,
):
    fsdp, seq = lax.axis_size("fsdp"), lax.axis_size("seq")
    devices = fsdp * seq
    rows = attn_blocks.shape[0]
    count = tokens.shape[2]
    length = seq * count
    heads = QUERY_HEADS // seq
    sharing = max(1, seq // KEY_VALUE_HEADS)
    all_rows = MICRO * length
    feed = FF // seq
    starts = piece_starts[:, 0]
    cosine, sine = rotary_tables(length)

    def gather_tokens(value):
        return lax.all_gather(value, "seq", axis=0, tiled=False)

    def sum_tokens(term):
        term = term.astype(BF16).reshape(seq, MICRO, count, D)
        return lax.psum_scatter(term, "seq", scatter_dimension=0, tiled=False).astype(F32)

    q_cut = D_BLK * QUERY_HEADS * HEAD_SIZE // PRECOND_ORDER
    kv_blk = D_BLK * KEY_VALUE_HEADS * HEAD_SIZE // PRECOND_ORDER
    k_cut, v_cut = q_cut + kv_blk, q_cut + 2 * kv_blk
    attn_low, ffn_low = attn_blocks.astype(BF16), ffn_blocks.astype(BF16)

    def shared_parts(shard):
        return jnp.repeat(column_parts(shard, seq // sharing), sharing, axis=0)

    chunk_rows = MICRO * count
    sizes = (fsdp, seq)
    lined = seq == 2 * LINE_CHIPS

    def chunked(value):
        return value.reshape(seq, chunk_rows, -1)

    def like_chunks(columns, dtype=BF16):
        return jax.ShapeDtypeStruct((seq, chunk_rows, columns), dtype)

    gain_all = lax.all_to_all(
        jnp.broadcast_to(gains.astype(BF16)[None], (devices,) + gains.shape),
        BOTH,
        split_axis=0,
        concat_axis=0,
        tiled=True,
    )
    gain_all = gain_all.transpose(1, 0, 2).reshape(2, D).astype(F32)
    qkv_parts = jnp.concatenate(
        [
            column_parts(attn_low[:, :q_cut], seq),
            shared_parts(attn_low[:, q_cut:k_cut]),
            shared_parts(attn_low[:, k_cut:v_cut]),
        ],
        axis=-1,
    )
    gu_cut = D_BLK * FF_BLK
    gu_parts = jnp.concatenate(
        [
            column_parts(ffn_low[:, :gu_cut], seq),
            column_parts(ffn_low[:, gu_cut : 2 * gu_cut], seq),
        ],
        axis=-1,
    )
    down_shard = ffn_low[:, 2 * gu_cut :].reshape(rows, FF_BLK, D_BLK, PRECOND_ORDER)
    out_shard = attn_low[:, v_cut:].reshape(rows, -1, D_BLK, PRECOND_ORDER)

    x = tokens[:, 0].astype(F32)
    inv_one = inverse_rms(x)
    cot_own = cotangent[:, 0].reshape(chunk_rows, D)
    if lined:
        qkv_w, down_w, gu_own, out_w, normed, qkv = exchange(
            0,
            sizes,
            own=tokens[:, 0].reshape(chunk_rows, D),
            keep=False,
            parts=(qkv_parts, down_shard.reshape(rows, FF_BLK, D).transpose(1, 0, 2)),
            wholes=(weight_shape(qkv_parts.shape[-1]), (PRECOND_ORDER, D)),
            in_vmem=(1, 0),
            directs=(("seq", "rows", gu_parts, (D_BLK, seq * rows, 2 * feed)),),
            out_part=out_shard.reshape(rows, -1, D).transpose(1, 0, 2),
            visit=norm_visit,
            extra_in=(gain_all,),
            extra_out=(like_chunks(D), like_chunks(qkv_parts.shape[-1], F32)),
        )
        qkv_w, normed = qkv_w.reshape(D, -1), normed.reshape(all_rows, D)
    else:
        qkv_w, out_w = gather_columns(qkv_parts), gather_rows(out_shard)
        x_all = gather_tokens(tokens[:, 0]).astype(F32)
        normed = (x_all * inverse_rms(x_all) * gain_all[0]).astype(BF16).reshape(all_rows, D)
        qkv = nn(normed, qkv_w)
    kept, mixed = attend(qkv.reshape(seq, MICRO, count, -1), starts, cosine, sine, heads)
    mixed = mixed.reshape(all_rows, heads * HEAD_SIZE)
    if lined:
        summed, cot_all, gu_w = exchange(
            1,
            sizes,
            own=cot_own,
            terms=(chunked(mixed), out_w),
            directs=(("fsdp", "spread", gu_own, weight_shape(2 * feed)),),
        )
        gu_w = gu_w.reshape(D, 2 * feed)
        cot_all, summed = cot_all.reshape(all_rows, D), summed.reshape(MICRO, count, D)
    else:
        gu_w, down_w = gather_columns(gu_parts), gather_rows(down_shard)
        cot_all = gather_tokens(cotangent[:, 0]).reshape(all_rows, D)
        summed = sum_tokens(nn(mixed, out_w))
    hidden = x + summed
    inv_two = inverse_rms(hidden)
    normed_two = (hidden * inv_two * gain_all[1]).astype(BF16)
    if lined:
        normed_two_all, inner, grad_gu = exchange(
            2,
            sizes,
            own=normed_two.reshape(chunk_rows, D),
            visit=feed_visit,
            extra_in=(chunked(cot_all), gu_w, down_w),
            extra_out=(like_chunks(feed), like_chunks(2 * feed)),
        )
        normed_two_all = normed_two_all.reshape(all_rows, D)
        inner, grad_gu = inner.reshape(all_rows, feed), grad_gu.reshape(all_rows, 2 * feed)
    else:
        normed_two_all = gather_tokens(normed_two).reshape(all_rows, D)
        gate_up = nn(normed_two_all, gu_w)
        gate, up = gate_up[:, :feed], gate_up[:, feed:]
        sigma = jax.nn.sigmoid(gate)
        inner = (gate * sigma * up).astype(BF16)
        grad_inner = nt(cot_all, down_w)
        grad_gu = jnp.concatenate(
            [
                (grad_inner * up * sigma * (1.0 + gate * (1.0 - sigma))).astype(BF16),
                (grad_inner * gate * sigma).astype(BF16),
            ],
            axis=1,
        )

    if lined:
        grad_norm_two, _, gu_term, down_parts = exchange(
            3,
            sizes,
            terms=(chunked(grad_gu), gu_w),
            transposed=True,
            feed_in=(chunked(normed_two_all), chunked(inner)),
            extra_in=(chunked(cot_all),),
        )
        grad_norm_two = grad_norm_two.reshape(MICRO, count, D)
        down_sum = sum_parts(down_parts).reshape(seq, rows, D)
    else:
        gu_sum = sum_columns(tn(normed_two_all, grad_gu).astype(BF16), rows)
        down_sum = sum_rows(tn(inner, cot_all).astype(BF16), rows)
        grad_norm_two = sum_tokens(nt(grad_gu, gu_w))
    gain_two = jnp.sum(grad_norm_two * hidden * inv_two, axis=(0, 1))
    grad_hidden = cotangent[:, 0].astype(F32) + norm_back(
        grad_norm_two, hidden, inv_two, gain_all[1]
    )
    grad_attn = grad_hidden.astype(BF16)
    if lined:
        summed, grad_attn_all, gu_parts, grad_mixed = exchange(
            4,
            sizes,
            own=grad_attn.reshape(chunk_rows, D),
            terms=(chunked(inner), down_w),
            directs=(("fsdp", "swap", gu_term, gu_term.shape),),
            visit=mixed_visit,
            extra_in=(out_w,),
            extra_out=(like_chunks(heads * HEAD_SIZE),),
        )
        gu_sum = sum_parts(gu_parts).reshape(D_BLK, seq, rows, 2 * feed)
        grad_attn_all, summed = grad_attn_all.reshape(all_rows, D), summed.reshape(MICRO, count, D)
    else:
        grad_attn_all = gather_tokens(grad_attn).reshape(all_rows, D)
        summed = sum_tokens(nn(inner, down_w))
        grad_mixed = nt(grad_attn_all, out_w).astype(BF16)
    block_out = (hidden + summed).astype(BF16)
    out_term = tn(mixed, grad_attn_all).astype(BF16)
    grad_mixed, down_sum, out_term = lax.optimization_barrier((grad_mixed, down_sum, out_term))
    gu_rows, down_rows = swap_columns(gu_sum), swap_rows(down_sum, rows)
    out_rows = swap_rows(sum_rows(out_term, rows), rows)
    grad_mixed = grad_mixed.reshape(seq, MICRO, count, -1)
    grad_q, grad_kv = attend_back(kept, grad_mixed, starts, cosine, sine, heads)
    if sharing > 1:
        groups = [[g * sharing + k for k in range(sharing)] for g in range(seq // sharing)]
        grad_kv = lax.psum(grad_kv, "seq", axis_index_groups=groups)
        grad_kv = jnp.where(lax.axis_index("seq") % sharing == 0, grad_kv, 0.0)
    grad_k, grad_v = grad_kv[..., :HEAD_SIZE], grad_kv[..., HEAD_SIZE:]
    half = HEAD_SIZE // 2
    swapped = jnp.concatenate([grad_k[..., half:], grad_k[..., :half]], axis=-1)
    table = (seq, 1, count, HEAD_SIZE)
    grad_k = grad_k * cosine.reshape(table) - swapped * sine.reshape(table)
    grad_qkv = jnp.concatenate([grad_q, grad_k.astype(BF16), grad_v.astype(BF16)], axis=-1)
    grad_qkv = grad_qkv.reshape(all_rows, -1)
    if lined:
        (grad_norm_one,) = exchange(5, sizes, terms=(chunked(grad_qkv), qkv_w), transposed=True)
        grad_norm_one = grad_norm_one.reshape(MICRO, count, D)
    else:
        grad_norm_one = sum_tokens(nt(grad_qkv, qkv_w))
    gain_one = jnp.sum(grad_norm_one * x * inv_one, axis=(0, 1))
    input_grad = (grad_hidden + norm_back(grad_norm_one, x, inv_one, gain_all[0])).astype(BF16)
    gain_terms = jnp.stack([gain_one, gain_two]).reshape(2, devices, -1).transpose(1, 0, 2)
    gain_grad = jnp.sum(
        lax.all_to_all(gain_terms, BOTH, split_axis=0, concat_axis=0, tiled=True), axis=0
    )
    qkv_rows = swap_columns(sum_columns(tn(normed, grad_qkv).astype(BF16), rows))

    def column_blocks(part):
        return part.transpose(2, 0, 1, 3).reshape(rows, -1, PRECOND_ORDER)

    def row_blocks(part):
        return part.transpose(1, 0, 2).reshape(rows, -1, PRECOND_ORDER)

    def shared_blocks(part):
        return column_blocks(part[:, ::sharing])

    q_width = heads * HEAD_SIZE
    attn_grad = jnp.concatenate(
        [
            column_blocks(qkv_rows[..., :q_width]),
            shared_blocks(qkv_rows[..., q_width : q_width + HEAD_SIZE]),
            shared_blocks(qkv_rows[..., q_width + HEAD_SIZE :]),
            row_blocks(out_rows),
        ],
        axis=1,
    )
    ffn_grad = jnp.concatenate(
        [
            column_blocks(gu_rows[..., :feed]),
            column_blocks(gu_rows[..., feed:]),
            row_blocks(down_rows),
        ],
        axis=1,
    )

    grad_all = jnp.concatenate([attn_grad, ffn_grad], axis=1)
    slots = left_stats.shape[0]
    blocks = grad_all.shape[1]
    slot_table = jnp.arange(slots)[:, None] + jnp.arange(devices)[None, :] * slots
    slot_match = owner_slot[None, None, :] == slot_table[:, :, None]
    slot_block = jnp.sum(jnp.where(slot_match, jnp.arange(blocks)[None, None, :], 0), axis=-1)
    filled = jnp.any(slot_match, axis=-1)
    by_block = jnp.transpose(grad_all, (1, 0, 2))
    outgoing = jnp.where(filled[:, :, None, None], by_block[slot_block], 0.0).astype(BF16)
    held = lax.all_to_all(outgoing, BOTH, split_axis=1, concat_axis=1, tiled=True)
    held = held.reshape(slots, PRECOND_ORDER, PRECOND_ORDER)
    own_slots = lax.axis_index(BOTH) * slots + jnp.arange(slots)
    owned = jnp.any(owner_slot[None, :] == own_slots[:, None], axis=-1)[:, None, None]

    def batched(a, b, a_dim, b_dim):
        return lax.dot_general(
            a, b, (((a_dim,), (b_dim,)), ((0,), (0,))), preferred_element_type=F32
        )

    step = batched(left_root.astype(BF16), held, 2, 1)
    step = batched(step.astype(BF16), right_root.astype(BF16), 2, 1).astype(BF16)
    returned = lax.all_to_all(
        step.reshape(slots, devices, rows, PRECOND_ORDER),
        BOTH,
        split_axis=1,
        concat_axis=1,
        tiled=True,
    )
    normalizer = 1.0 * MICRO * fsdp * length * PRECOND_ORDER
    gram_left = batched(held, held, 2, 2) / normalizer
    gram_right = batched(held, held, 1, 1) / normalizer
    new_left = jnp.where(
        owned, STAT_DECAY * left_stats + (1.0 - STAT_DECAY) * gram_left, left_stats
    )
    new_right = jnp.where(
        owned, STAT_DECAY * right_stats + (1.0 - STAT_DECAY) * gram_right, right_stats
    )
    flat = jnp.transpose(returned, (1, 0, 2, 3)).reshape(devices * slots, rows, PRECOND_ORDER)
    update = jnp.transpose(flat[owner_slot], (1, 0, 2)).astype(F32)
    attn_count = attn_blocks.shape[1]
    return (
        block_out[:, None],
        input_grad[:, None],
        attn_grad.astype(F32),
        ffn_grad.astype(F32),
        gain_grad,
        attn_blocks - STEP_RATE * update[:, :attn_count],
        ffn_blocks - STEP_RATE * update[:, attn_count:],
        gains - GAIN_RATE * gain_grad,
        new_left,
        new_right,
    )


def solution(mesh):
    by_token = P(None, "fsdp", "seq", None)
    by_row = P(BOTH, None, None)
    by_gain = P(None, BOTH)
    return jax.shard_map(
        shards,
        mesh=mesh,
        in_specs=(
            by_token,
            by_token,
            P(None, "fsdp", None),
            by_row,
            by_row,
            by_gain,
            by_row,
            by_row,
            by_row,
            by_row,
            P(),
        ),
        out_specs=(
            by_token,
            by_token,
            by_row,
            by_row,
            by_gain,
            by_row,
            by_row,
            by_gain,
            by_row,
            by_row,
        ),
        check_vma=False,
    )
```
